512 devices in a mesh: row: 16 (over x, y_lo, core), col: 32 (over z, y_hi).
Axes of the slice: x: 4, y: 4 (y_hi: 2, y_lo: 2; y = y_hi * 2 + y_lo), z: 16, core: 2. Of those that a mesh axis runs over, the one named last changes fastest.
Arguments:
- features: bfloat16 [128, 1024, 256], P('row', 'col'), may hold values from -16 to 16
- expand_weight: bfloat16 [2, 256, 1024], replicated, may hold values from -0.375 to 0.375
- expand_bias: float32 [2, 1024], replicated, may hold values from -3 to 3
- depth_weight: float32 [2, 3, 3, 1024], replicated, may hold values from -2 to 2
- depth_bias: float32 [2, 1024], replicated, may hold values from -3 to 3
- project_weight: bfloat16 [2, 1024, 256], replicated, may hold values from -0.1875 to 0.1875
- project_bias: float32 [2, 256], replicated, may hold values from -3 to 3
- qkv_weight: bfloat16 [2, 256, 768], replicated, may hold values from -0.375 to 0.375
- aggregate_depth: float32 [2, 5, 5, 768], replicated, may hold values from -1.25 to 1.25
- aggregate_group: bfloat16 [2, 24, 32, 32], replicated, may hold values from -1 to 1
- output_weight: bfloat16 [2, 512, 256], replicated, may hold values from -0.25 to 0.25
- output_bias: float32 [2, 256], replicated, may hold values from -3 to 3
- head_weight: bfloat16 [3, 3, 4, 256], replicated, may hold values from -0.125 to 0.125
- head_bias: float32 [4], replicated, may hold values from -3 to 3
Outputs:
- final_map: bfloat16 [128, 1024, 256], P('row', 'col')
- boxes: float32 [4, 128, 1024], P(None, 'row', 'col')
The draws below stay inside these ranges and needn't reach their ends.
All inputs are finite; a program needn't handle non-finite values.
Results may differ from the reference program's by a relative error of at most 0.009.
Values may be sent and summed in bfloat16 or wider, within the bound.
A program may use at most 64 MiB of HBM per device.

```python
import jax
import jax.numpy as jnp
from jax import lax

C = 256
HD = 32
HEADS = 8
E = 1024
SECTIONS = 2
TH = 8
TW = 32
NH = 128
NW = 1024
N_ROW = 16


def draw_features(key, part):
    key_base, key_rows, key_cols, key_tile_scale, key_tile_offset = jax.random.split(key, 5)
    tile_rows = NH // TH
    tile_cols = NW // TW
    row_scale = jnp.exp(jax.random.uniform(key_rows, (NH, 1, 1), jnp.float32, -0.57, 0.57))
    col_scale = jnp.exp(jax.random.uniform(key_cols, (1, NW, 1), jnp.float32, -0.57, 0.57))
    tile_scale = jnp.exp(jax.random.uniform(key_tile_scale, (tile_rows, tile_cols, 1), jnp.float32, -1.2, 1.2))
    tile_offset = jnp.clip(jax.random.normal(key_tile_offset, (tile_rows, tile_cols, C), jnp.float32), -2.5, 2.5)
    scale_map = jnp.repeat(jnp.repeat(tile_scale, TH, axis=0), TW, axis=1)
    offset_map = jnp.repeat(jnp.repeat(tile_offset, TH, axis=0), TW, axis=1)
    base = jnp.clip(jax.random.normal(key_base, (NH, NW, C), jnp.float32), -4.0, 4.0)
    value = (base * row_scale * col_scale + offset_map) * scale_map
    return jnp.clip(value, -16.0, 16.0).astype(jnp.bfloat16)


def centred(rng, shape, deviation, most, kind=jnp.bfloat16):
    return jnp.clip(deviation * jax.random.normal(rng, shape, jnp.float32), -most, most).astype(kind)


def setup_inputs(seed: int = 0) -> dict:
    splits = jax.random.split(jax.random.key(seed), 15)
    features = draw_features(jax.random.fold_in(splits[14], 71), 0)
    expand_weight = centred(splits[1], (SECTIONS, C, E), C ** -0.5, 0.375)
    expand_bias = centred(splits[2], (SECTIONS, E), 0.5, 3.0, jnp.float32)
    depth_weight = centred(splits[3], (SECTIONS, 3, 3, E), 9 ** -0.5, 2.0, jnp.float32)
    depth_bias = centred(splits[4], (SECTIONS, E), 0.5, 3.0, jnp.float32)
    project_weight = centred(splits[5], (SECTIONS, E, C), E ** -0.5, 0.1875)
    project_bias = centred(splits[6], (SECTIONS, C), 0.5, 3.0, jnp.float32)
    qkv_weight = centred(splits[7], (SECTIONS, C, 3 * C), C ** -0.5, 0.375)
    aggregate_depth = centred(splits[8], (SECTIONS, 5, 5, 3 * C), 25 ** -0.5, 1.25, jnp.float32)
    aggregate_group = centred(splits[9], (SECTIONS, 3 * HEADS, HD, HD), HD ** -0.5, 1.0)
    output_weight = centred(splits[10], (SECTIONS, 2 * C, C), (2 * C) ** -0.5, 0.25)
    output_bias = centred(splits[11], (SECTIONS, C), 0.5, 3.0, jnp.float32)
    head_weight = centred(splits[12], (3, 3, 4, C), (9 * C) ** -0.5, 0.125)
    head_bias = centred(splits[13], (4,), 1.0, 3.0, jnp.float32)
    return {"features": features, "expand_weight": expand_weight, "expand_bias": expand_bias, "depth_weight": depth_weight, "depth_bias": depth_bias, "project_weight": project_weight, "project_bias": project_bias, "qkv_weight": qkv_weight, "aggregate_depth": aggregate_depth, "aggregate_group": aggregate_group, "output_weight": output_weight, "output_bias": output_bias, "head_weight": head_weight, "head_bias": head_bias}


def hard_swish(value):
    return value * jnp.minimum(jnp.maximum(value + 3.0, 0.0), 6.0) / 6.0


def depthwise(padded, weight, rows, cols):
    ksize = weight.shape[0]
    total = jnp.zeros((rows, cols, padded.shape[2]), jnp.float32)
    for offset_r in range(ksize):
        for offset_c in range(ksize):
            total = total + padded[offset_r:offset_r + rows, offset_c:offset_c + cols, :].astype(jnp.float32) * weight[offset_r, offset_c]
    return total


def dense(values, weight):
    flat = values.reshape(-1, values.shape[-1])
    result = jnp.dot(flat, weight, preferred_element_type=jnp.float32)
    return result.reshape(values.shape[:-1] + (weight.shape[1],))


def heads_of(padded_qkv, agg_depth, agg_group, rows, cols, heads, head_dim):
    center = padded_qkv[2:2 + rows, 2:2 + cols, :]
    spread = depthwise(padded_qkv, agg_depth, rows, cols).astype(jnp.bfloat16)
    grouped = jnp.einsum("rcgd,gde->rcge", spread.reshape(rows, cols, 3 * heads, head_dim).astype(jnp.float32), agg_group.astype(jnp.float32), precision=lax.Precision.HIGHEST).astype(jnp.bfloat16)
    return jnp.concatenate([center.reshape(rows, cols, heads, 3, head_dim), grouped.reshape(rows, cols, heads, 3, head_dim)], axis=2)


def reference(features, expand_weight, expand_bias, depth_weight, depth_bias, project_weight, project_bias, qkv_weight, aggregate_depth, aggregate_group, output_weight, output_bias, head_weight, head_bias):
    current = features
    block_ids = jnp.arange(N_ROW, dtype=jnp.int32)
    col_at = jnp.arange(NW + 2, dtype=jnp.int32)
    col_ok = ((col_at >= 1) & (col_at <= NW)).astype(jnp.bfloat16)
    for section in range(SECTIONS):
        padded = jnp.pad(current, ((1, 1), (1, 1), (0, 0)))

        def mb_block(index, current=current, padded=padded, section=section):
            start = index * TH
            piece = lax.dynamic_slice_in_dim(padded, start, TH + 2, 0)
            hidden = hard_swish(dense(piece, expand_weight[section]) + expand_bias[section]).astype(jnp.bfloat16)
            row_at = start + jnp.arange(TH + 2, dtype=jnp.int32)
            row_ok = ((row_at >= 1) & (row_at <= NH)).astype(jnp.bfloat16)
            hidden = hidden * row_ok[:, None, None] * col_ok[None, :, None]
            spread = hard_swish(depthwise(hidden, depth_weight[section], TH, NW) + depth_bias[section]).astype(jnp.bfloat16)
            base = lax.dynamic_slice_in_dim(current, start, TH, 0)
            return (base + dense(spread, project_weight[section]) + project_bias[section]).astype(jnp.bfloat16)

        mixed = lax.map(mb_block, block_ids).reshape(NH, NW, C)
        padded_mixed = jnp.pad(mixed, ((2, 2), (2, 2), (0, 0)))

        def heads_block(index, padded_mixed=padded_mixed, section=section):
            piece = lax.dynamic_slice_in_dim(padded_mixed, index * TH, TH + 4, 0)
            qkv = dense(piece, qkv_weight[section]).astype(jnp.bfloat16)
            return heads_of(qkv, aggregate_depth[section], aggregate_group[section], TH, NW, HEADS, HD)

        def summary_block(index):
            both = heads_block(index)
            keys = jax.nn.relu(both[:, :, :, 1, :]).astype(jnp.float32)
            values = both[:, :, :, 2, :].astype(jnp.float32)
            kv = jnp.einsum("rchd,rche->hde", keys, values, precision=lax.Precision.HIGHEST)
            return kv, jnp.sum(keys, axis=(0, 1))

        kv_parts, key_parts = lax.map(summary_block, block_ids)
        kv_all = jnp.sum(kv_parts, axis=0)
        key_all = jnp.sum(key_parts, axis=0)

        def apply_block(index, mixed=mixed, section=section, kv_all=kv_all, key_all=key_all):
            both = heads_block(index)
            queries = jax.nn.relu(both[:, :, :, 0, :]).astype(jnp.float32)
            numer = jnp.einsum("rchd,hde->rche", queries, kv_all, precision=lax.Precision.HIGHEST)
            denom = jnp.einsum("rchd,hd->rch", queries, key_all, precision=lax.Precision.HIGHEST)
            attended = (numer / (denom[..., None] + 1e-6)).astype(jnp.bfloat16).reshape(TH, NW, 2 * C)
            base = lax.dynamic_slice_in_dim(mixed, index * TH, TH, 0)
            return (base + dense(attended, output_weight[section]) + output_bias[section]).astype(jnp.bfloat16)

        current = lax.map(apply_block, block_ids).reshape(NH, NW, C)
    padded = jnp.pad(current, ((1, 1), (1, 1), (0, 0)))
    total = jnp.zeros((NH * NW, 4), jnp.float32)
    for offset_r in range(3):
        for offset_c in range(3):
            window = padded[offset_r:offset_r + NH, offset_c:offset_c + NW, :].reshape(NH * NW, C)
            total = total + jnp.dot(window, head_weight[offset_r, offset_c].T, preferred_element_type=jnp.float32)
    boxes = total.T.reshape(4, NH, NW) + head_bias[:, None, None]
    return current, boxes
```

```python
import functools

import jax
import jax.numpy as jnp
from jax import lax
from jax.experimental import pallas as pl
from jax.experimental.pallas import tpu as pltpu
from jax.sharding import PartitionSpec as P

MESH = pl.DeviceIdType.MESH
F32 = jnp.float32
BF16 = jnp.bfloat16
ROWS = 8
COLS = 32
PITCH = 40
WIDTH = 256
EXPANDED = 1024
CHUNK = 256
HD = 32
HEADS = 8
HALOS = (3, 1)


def spot():
    return lax.axis_index("row"), lax.axis_index("col")


def beside(dr, dc):
    r, c = spot()
    return lax.rem(r + 16 + dr, 16), lax.rem(c + 32 + dc, 32)


def far_first(k, half):
    return half + (1 - 2 * lax.rem(k, 2)) * ((k + 1) // 2)


def plane_of(r, c):
    return r * 2 + lax.rem(c, 2)


def plane_peer(k):
    r, c = spot()
    dx = far_first(k // 8, 2)
    dy = far_first(lax.rem(k // 2, 4), 2)
    dk = 1 - lax.rem(k, 2)
    x = lax.rem(r // 4 + dx, 4)
    y = lax.rem(lax.rem(c, 2) * 2 + lax.rem(r // 2, 2) + dy, 4)
    core = lax.rem(r + dk, 2)
    return x * 4 + lax.rem(y, 2) * 2 + core, (c // 2) * 2 + y // 2


def depth_peer(k):
    r, c = spot()
    z = lax.rem(c // 2 + far_first(k, 8), 16)
    return r, z * 2 + lax.rem(c, 2)


AROUND = [(-1, 0), (1, 0), (0, -1), (0, 1), (-1, -1), (-1, 1), (1, -1), (1, 1)]


def each(count, body):
    def step(k, carry):
        body(k)
        return carry

    lax.fori_loop(0, count, step, 0)


def enter():
    barrier = pltpu.get_barrier_semaphore()

    def tell(device):
        pl.semaphore_signal(barrier, inc=1, device_id=device, device_id_type=MESH)

    each(15, lambda k: tell(depth_peer(k)))
    each(31, lambda k: tell(plane_peer(k)))
    for dr, dc in AROUND:
        tell(beside(dr, dc))


def entered():
    pl.semaphore_wait(pltpu.get_barrier_semaphore(), 15 + 31 + 8)


def dot(a, b):
    return jnp.dot(a, b, preferred_element_type=F32)


def gate(v):
    return v * jnp.minimum(jnp.maximum(v + 3.0, 0.0), 6.0)


def inside(rows, halo, lanes):
    r, c = spot()
    at = lax.broadcasted_iota(jnp.int32, (rows * PITCH, lanes), 0)
    row = at // PITCH
    col = at - row * PITCH
    row = row + (r * ROWS - halo)
    col = col + (c * COLS - halo)
    ok = (row >= 0) & (row < 128) & (col >= 0) & (col < 1024)
    return jnp.where(ok, 1.0, 0.0).astype(F32)


def pack(tile, left, right, packed, wide):
    for r in range(ROWS):
        row = tile(r)
        packed[0, 4 * r : 4 * r + 4, :wide] = row[0:4]
        packed[1, 4 * r : 4 * r + 4, :wide] = row[COLS - 4 : COLS]
    left[...] = packed[0, :, :wide].astype(BF16)
    right[...] = packed[1, :, :wide].astype(BF16)


def trade(tile, left, right, halo, across, sides, corners, send, recv):
    low = tile.at[pl.ds(ROWS - halo, halo)]
    high = tile.at[pl.ds(0, halo)]
    top = pl.ds(0, 16)
    bottom = pl.ds(16, 16)
    plan = [
        ((1, 0), low, across.at[0]),
        ((-1, 0), high, across.at[1]),
        ((0, 1), right, sides.at[0]),
        ((0, -1), left, sides.at[1]),
        ((1, 1), right.at[bottom], corners.at[0]),
        ((1, -1), left.at[bottom], corners.at[1]),
        ((-1, 1), right.at[top], corners.at[2]),
        ((-1, -1), left.at[top], corners.at[3]),
    ]
    return [
        pltpu.make_async_remote_copy(
            src_ref=src,
            dst_ref=dst,
            send_sem=send.at[i],
            recv_sem=recv.at[i],
            device_id=beside(*where),
            device_id_type=MESH,
        )
        for i, (where, src, dst) in enumerate(plan)
    ]


def assemble(out, tile, halo, across, sides, corners):
    wide = out.shape[1]
    skip = 4 - halo
    ends = halo + COLS

    def put(row, col, value):
        start = row * PITCH + col
        out[start : start + value.shape[0], :] = value

    for r in range(ROWS):
        put(halo + r, halo, tile[r].astype(F32))
    for r in range(halo):
        put(r, halo, across[0, r].astype(F32))
        put(halo + ROWS + r, halo, across[1, r].astype(F32))
    west = sides[0].astype(F32)
    east = sides[1].astype(F32)
    for r in range(ROWS):
        put(halo + r, 0, west[4 * r + skip : 4 * r + 4])
        put(halo + r, ends, east[4 * r : 4 * r + halo])
    nw, ne, sw, se = [corners[i].astype(F32) for i in range(4)]
    for r in range(halo):
        low = 4 * (r + skip)
        put(r, 0, nw[low + skip : low + 4])
        put(r, ends, ne[low : low + halo])
        put(halo + ROWS + r, 0, sw[4 * r + skip : 4 * r + 4])
        put(halo + ROWS + r, ends, se[4 * r : 4 * r + halo])


def prepare(s, qkv_weight, agg_depth, agg_group, qkv_w, agg_w, grp_w, stack):
    i = lax.broadcasted_iota(jnp.int32, (3 * WIDTH, 3 * WIDTH), 0)
    j = lax.broadcasted_iota(jnp.int32, (3 * WIDTH, 3 * WIDTH), 1)
    kind = j // WIDTH
    head = (j - kind * WIDTH) // HD
    lane = j - (j // HD) * HD
    order = jnp.where(i == head * (3 * HD) + kind * HD + lane, 1.0, 0.0).astype(BF16)
    qkv_w[s] = dot(qkv_weight[s], order).astype(BF16)
    stack[...] = jnp.zeros_like(stack)
    for a in range(5):
        full = agg_depth[s, a]
        high = full.astype(BF16).astype(F32)
        rest = full - high
        mid = rest.astype(BF16).astype(F32)
        stack[8 * a : 8 * a + 5] = high
        stack[48 + 8 * a : 48 + 8 * a + 5] = mid
        stack[96 + 8 * a : 96 + 8 * a + 5] = rest - mid
    moved = dot(stack[...].astype(BF16), order)
    agg_w[s] = moved[0:48] + moved[48:96] + moved[96:144]
    i = lax.broadcasted_iota(jnp.int32, (HD, WIDTH), 0)
    j = lax.broadcasted_iota(jnp.int32, (HD, WIDTH), 1)
    spread = jnp.where(i == j - (j // HD) * HD, 1.0, 0.0).astype(BF16)
    i = lax.broadcasted_iota(jnp.int32, (WIDTH, WIDTH), 0)
    j = lax.broadcasted_iota(jnp.int32, (WIDTH, WIDTH), 1)
    same = i // HD == j // HD
    for t in range(3):
        rows = jnp.concatenate([agg_group[s, 3 * h + t] for h in range(HEADS)], axis=0)
        grp_w[s, t] = jnp.where(same, dot(rows, spread), 0.0).astype(BF16)


def kernel(
    features,
    expand_weight,
    expand_bias,
    depth_weight,
    depth_bias,
    project_weight,
    project_bias,
    qkv_weight,
    agg_depth,
    agg_group,
    output_weight,
    output_bias,
    head_weight,
    head_bias,
    out_map,
    out_boxes,
    xp,
    xb,
    edge3,
    edge2,
    hidden,
    spread,
    acc,
    qkv,
    scaled,
    center,
    mixed,
    joined,
    qkv_w,
    agg_w,
    grp_w,
    stack,
    head_w,
    packed,
    lefts,
    rights,
    f_left,
    f_right,
    tile,
    f_across,
    f_sides,
    f_corners,
    across3,
    across1,
    sides,
    corners,
    part,
    got,
    mine,
    deep,
    total,
    whole,
    table,
    keys,
    hs_send,
    hs_recv,
    ar_send,
    ar_recv,
):
    enter()
    pack(
        lambda r: features[r].astype(F32), f_left, f_right, packed, WIDTH
    )
    for s in range(2):
        prepare(s, qkv_weight, agg_depth, agg_group, qkv_w, agg_w, grp_w, stack)
    head_w[...] = jnp.zeros_like(head_w)
    for a in range(3):
        for b in range(3):
            at = 8 * (3 * a + b)
            head_w[at : at + 4] = head_weight[a, b].astype(F32)
    edge3[...] = inside(14, 3, 128) * (1.0 / 6.0)
    edge2[...] = inside(12, 2, 128)
    xp[...] = jnp.zeros_like(xp)
    joined[...] = jnp.zeros_like(joined)
    part[...] = jnp.zeros_like(part)
    entered()

    first = trade(
        features, f_left, f_right, 3, f_across, f_sides, f_corners, hs_send.at[2], hs_recv.at[2]
    )
    for copy in first:
        copy.start()
    for copy in first:
        copy.wait()
    assemble(xp, features, 3, f_across, f_sides, f_corners)
    xb[...] = xp[...].astype(BF16)

    for s in range(2):
        halo = HALOS[s]
        acc[...] = jnp.zeros_like(acc)

        def expand(c, carry, s=s):
            wide = pl.ds(pl.multiple_of(c * CHUNK, CHUNK), CHUNK)
            value = gate(dot(xb[...], expand_weight[s, :, wide]) + expand_bias[s : s + 1, wide])
            for l in range(CHUNK // 128):
                hidden[:, 128 * l : 128 * l + 128] = (
                    value[:, 128 * l : 128 * l + 128] * edge3[...]
                )
            for l in range(CHUNK // 128):
                here = slice(128 * l, 128 * l + 128)
                lanes = pl.ds(pl.multiple_of(c * CHUNK + 128 * l, 128), 128)
                taps = [
                    [depth_weight[s, a, b : b + 1, lanes] for b in range(3)] for a in range(3)
                ]
                bias = depth_bias[s : s + 1, lanes]
                for pair in range(6):
                    done = []
                    for r in (2 * pair, 2 * pair + 1):
                        rows = [
                            hidden[PITCH * (r + a) : PITCH * (r + a) + PITCH, here]
                            for a in range(3)
                        ]
                        cols = [
                            rows[0] * taps[0][b] + rows[1] * taps[1][b] + rows[2] * taps[2][b]
                            for b in range(3)
                        ]
                        value = (
                            cols[0]
                            + pltpu.roll(cols[1], PITCH - 1, 0)
                            + pltpu.roll(cols[2], PITCH - 2, 0)
                            + bias
                        )
                        done.append(gate(value) * (1.0 / 6.0))
                    spread[2 * PITCH * pair : 2 * PITCH * (pair + 1), here] = jnp.concatenate(
                        done, axis=0
                    ).astype(BF16)
            acc[...] += dot(spread[...], project_weight[s, wide, :])
            return carry

        lax.fori_loop(0, EXPANDED // CHUNK, expand, 0)
        bias = project_bias[s : s + 1]
        for r in range(12):
            here = slice(PITCH * r, PITCH * r + PITCH)
            base = xp[PITCH * (r + 1) : PITCH * (r + 2)]
            value = acc[here] + pltpu.roll(base, PITCH - 1, 0) + bias
            for l in range(WIDTH // 128):
                lanes = slice(128 * l, 128 * l + 128)
                mixed[here, lanes] = value[:, lanes] * edge2[here]
        qkv[...] = dot(mixed[...].astype(BF16), qkv_w[s])

        def taps5(l, carry, s=s):
            lanes = pl.ds(pl.multiple_of(l * 128, 128), 128)
            for r in range(ROWS):
                cols = [None] * 5
                for a in range(5):
                    row = qkv[PITCH * (r + a) : PITCH * (r + a) + PITCH, lanes]
                    for b in range(5):
                        term = row * agg_w[s, 8 * a + b : 8 * a + b + 1, lanes]
                        cols[b] = term if a == 0 else cols[b] + term
                value = cols[0]
                for b in range(1, 5):
                    value = value + pltpu.roll(cols[b], PITCH - b, 0)
                scaled[COLS * r : COLS * r + COLS, lanes] = value[0:COLS].astype(BF16)
                near = pltpu.roll(qkv[PITCH * (r + 2) : PITCH * (r + 3), lanes], PITCH - 2, 0)
                center[COLS * r : COLS * r + COLS, lanes] = near[0:COLS].astype(BF16)
            return carry

        def kind(t):
            lanes = slice(WIDTH * t, WIDTH * t + WIDTH)
            return [center[:, lanes], dot(scaled[:, lanes], grp_w[s, t]).astype(BF16)]

        lax.fori_loop(2, 6, taps5, 0)
        lane = lax.broadcasted_iota(jnp.int32, (HD, 128), 1) // HD
        ones = jnp.ones((16, ROWS * COLS), BF16)
        for branch, (k, v) in enumerate(zip(kind(1), kind(2))):
            k = jnp.maximum(k, jnp.zeros_like(k))
            outer = lax.dot_general(k, v, (((0,), (0,)), ((), ())), preferred_element_type=F32)
            count = dot(ones, k)
            for g in range(2):
                group = 2 * branch + g
                lanes = slice(128 * g, 128 * g + 128)
                fold = jnp.zeros((HD, 128), F32)
                for h in range(4):
                    low = 128 * g + HD * h
                    fold = jnp.where(lane == h, outer[low : low + HD, lanes], fold)
                for p in range(8):
                    part[s, 8 * group + p, 0:4, :] = fold[4 * p : 4 * p + 4]
                part[s, group, 4:5, :] = count[0:1, lanes]

        me = plane_of(*spot())
        depth = spot()[1] // 2

        def remote(src, dst, stage, device):
            return pltpu.make_async_remote_copy(
                src_ref=src,
                dst_ref=dst,
                send_sem=ar_send.at[s, stage],
                recv_sem=ar_recv.at[s, stage],
                device_id=device,
                device_id_type=MESH,
            )

        def send1(k, s=s):
            device = plane_peer(k)
            remote(part.at[s, plane_of(*device)], got.at[s, me], 0, device).start()

        def send2(k, s=s):
            remote(mine.at[s], deep.at[s, depth], 1, depth_peer(k)).start()

        def send3(k, s=s):
            remote(total.at[s], whole.at[s, me], 2, plane_peer(k)).start()

        def arrived(buffer, count, stage, s=s):
            view = buffer.at[s, pl.ds(0, count)]
            pltpu.make_async_copy(view, view, ar_recv.at[s, stage]).wait()

        def sent(buffer, count, stage, s=s):
            view = buffer.at[s, pl.ds(0, count)]
            pltpu.make_async_copy(view, view, ar_send.at[s, stage]).wait()

        each(31, send1)
        got[s, me] = part[s, me]

        lax.fori_loop(0, 2, taps5, 0)
        near, far = kind(0)
        for r in range(ROWS):
            here = slice(COLS * r, COLS * r + COLS)
            value = pltpu.roll(mixed[PITCH * (r + 2) : PITCH * (r + 3)], PITCH - 2, 0)
            tile[s, r, :, 0:WIDTH] = value[0:COLS].astype(BF16)
            tile[s, r, :, WIDTH : 2 * WIDTH] = jnp.maximum(near[here], jnp.zeros_like(near[here]))
            tile[s, r, :, 2 * WIDTH :] = jnp.maximum(far[here], jnp.zeros_like(far[here]))
        pack(
            lambda r, s=s: tile[s, r].astype(F32), lefts.at[s], rights.at[s], packed, 3 * WIDTH
        )
        across = across3 if halo == 3 else across1
        swap = trade(
            tile.at[s],
            lefts.at[s],
            rights.at[s],
            halo,
            across,
            sides.at[s],
            corners.at[s],
            hs_send.at[s],
            hs_recv.at[s],
        )

        arrived(got, 31, 0)
        mine[s] = jnp.sum(got[s], axis=0)
        each(15, send2)
        deep[s, depth] = mine[s]
        for copy in swap:
            copy.start()
        for copy in swap:
            copy.wait()
        area = (ROWS + 2 * halo) * PITCH
        assemble(joined.at[pl.ds(0, area)], tile.at[s], halo, across, sides.at[s], corners.at[s])
        arrived(deep, 15, 1)
        total[s] = jnp.sum(deep[s], axis=0)
        each(31, send3)
        whole[s, me] = total[s]
        arrived(whole, 31, 2)
        sent(got, 31, 0)
        sent(deep, 15, 1)
        sent(whole, 31, 2)

        for p in range(32):
            table[4 * p : 4 * p + 4, :] = whole[s, p, 0:4, :]
        i = lax.broadcasted_iota(jnp.int32, (WIDTH, WIDTH), 0)
        j = lax.broadcasted_iota(jnp.int32, (WIDTH, WIDTH), 1)
        same = i // HD == j // HD
        ones = jnp.where(same, 1.0, 0.0).astype(BF16)
        attended = []
        for branch in range(2):
            blocks = []
            for g in range(2):
                group = 2 * branch + g
                block = table[HD * group : HD * group + HD]
                blocks.append(jnp.concatenate([block] * 4, axis=0))
                keys[0:1, 128 * g : 128 * g + 128] = whole[s, group, 4:5, :]
            numer_w = jnp.where(
                same, jnp.concatenate([jnp.concatenate([b, b], axis=1) for b in blocks], axis=0), 0.0
            )
            key_row = jnp.broadcast_to(keys[0:1, :], (WIDTH, WIDTH))
            denom_w = dot(jnp.where(i == j, key_row, 0.0).astype(BF16), ones)
            q = joined[0:area, WIDTH * (1 + branch) : WIDTH * (2 + branch)].astype(BF16)
            numer = dot(q, numer_w.astype(BF16))
            denom = dot(q, denom_w.astype(BF16))
            attended.append((numer / (denom + 1e-06)).astype(BF16))
        value = (
            joined[0:area, 0:WIDTH]
            + dot(attended[0], output_weight[s, 0:WIDTH])
            + dot(attended[1], output_weight[s, WIDTH:])
            + output_bias[s : s + 1]
        )
        xp[0:area] = value
        xb[0:area] = value.astype(BF16)

    for r in range(ROWS):
        start = PITCH * (r + 1) + 1
        out_map[r] = xp[start : start + COLS].astype(BF16)
    area = 10 * PITCH
    on_map = inside(10, 1, 128)
    final = jnp.concatenate(
        [
            (xp[0:area, 128 * l : 128 * l + 128] * on_map).astype(BF16)
            for l in range(WIDTH // 128)
        ],
        axis=1,
    )
    final = jnp.concatenate([final, jnp.zeros((512 - area, WIDTH), BF16)], axis=0)
    taps = lax.dot_general(
        head_w[...].astype(BF16), final, (((1,), (1,)), ((), ())), preferred_element_type=F32
    )
    boxes = jnp.zeros((8, 512), F32)
    for a in range(3):
        for b in range(3):
            at = 8 * (3 * a + b)
            shift = PITCH * a + b
            term = taps[at : at + 8]
            boxes = boxes + (term if shift == 0 else pltpu.roll(term, 512 - shift, 1))
    for r in range(ROWS):
        row = boxes if r == 0 else pltpu.roll(boxes, 512 - PITCH * r, 1)
        for o in range(4):
            out_boxes[o, r : r + 1, :] = row[o : o + 1, 0:COLS] + head_bias[o]


def local(*args):
    dma = pltpu.SemaphoreType.DMA
    vmem = pltpu.VMEM
    area = 14 * PITCH
    inner = 12 * PITCH
    wide = 3 * WIDTH
    scratch = [
        vmem((area, WIDTH), F32),
        vmem((area, WIDTH), BF16),
        vmem((area, 128), F32),
        vmem((inner, 128), F32),
        vmem((area, CHUNK), F32),
        vmem((inner, CHUNK), BF16),
        vmem((inner, WIDTH), F32),
        vmem((inner, wide), F32),
        vmem((ROWS * COLS, wide), BF16),
        vmem((ROWS * COLS, wide), BF16),
        vmem((inner, WIDTH), F32),
        vmem((area, wide), F32),
        vmem((2, WIDTH, wide), BF16),
        vmem((2, 48, wide), F32),
        vmem((2, 3, WIDTH, WIDTH), BF16),
        vmem((144, wide), F32),
        vmem((72, WIDTH), F32),
        vmem((2, 32, wide), F32),
        vmem((2, 32, wide), BF16),
        vmem((2, 32, wide), BF16),
        vmem((32, WIDTH), BF16),
        vmem((32, WIDTH), BF16),
        vmem((2, ROWS, COLS, wide), BF16),
        vmem((2, 3, COLS, WIDTH), BF16),
        vmem((2, 32, WIDTH), BF16),
        vmem((4, 16, WIDTH), BF16),
        vmem((2, 3, COLS, wide), BF16),
        vmem((2, 1, COLS, wide), BF16),
        vmem((2, 2, 32, wide), BF16),
        vmem((2, 4, 16, wide), BF16),
        vmem((2, 32, 5, 128), F32),
        vmem((2, 32, 5, 128), F32),
        vmem((2, 5, 128), F32),
        vmem((2, 16, 5, 128), F32),
        vmem((2, 5, 128), F32),
        vmem((2, 32, 5, 128), F32),
        vmem((128, 128), F32),
        vmem((8, WIDTH), F32),
        dma((3, 8)),
        dma((3, 8)),
        dma((2, 3)),
        dma((2, 3)),
    ]
    in_vmem = pl.BlockSpec(memory_space=pltpu.VMEM)
    return pl.pallas_call(
        kernel,
        out_shape=(
            jax.ShapeDtypeStruct((ROWS, COLS, WIDTH), BF16),
            jax.ShapeDtypeStruct((4, ROWS, COLS), F32),
        ),
        in_specs=[in_vmem] * 13 + [pl.BlockSpec(memory_space=pltpu.SMEM)],
        out_specs=(in_vmem, in_vmem),
        scratch_shapes=scratch,
        compiler_params=pltpu.CompilerParams(
            collective_id=0, has_side_effects=True, vmem_limit_bytes=48 * 1024 * 1024
        ),
    )(*args)


def solution(mesh):
    return jax.shard_map(
        local,
        mesh=mesh,
        in_specs=(P("row", "col", None),) + (P(),) * 13,
        out_specs=(P("row", "col", None), P(None, "row", "col")),
        check_vma=False,
    )
```

```python
import functools

import jax
import jax.numpy as jnp
from jax import lax
from jax.experimental import pallas as pl
from jax.experimental.pallas import tpu as pltpu
from jax.sharding import PartitionSpec as P

MESH = pl.DeviceIdType.MESH
F32 = jnp.float32
BF16 = jnp.bfloat16
ROWS = 8
COLS = 32
PITCH = 40
WIDTH = 256
EXPANDED = 1024
CHUNK = 256
HD = 32
HEADS = 8
HALOS = (3, 1)


def spot():
    return lax.axis_index("row"), lax.axis_index("col")


def beside(dr, dc):
    r, c = spot()
    return lax.rem(r + 16 + dr, 16), lax.rem(c + 32 + dc, 32)


def far_first(k, half):
    return half + (1 - 2 * lax.rem(k, 2)) * ((k + 1) // 2)


def plane_of(r, c):
    return r * 2 + lax.rem(c, 2)


def plane_peer(k):
    r, c = spot()
    dx = far_first(k // 8, 2)
    dy = far_first(lax.rem(k // 2, 4), 2)
    dk = 1 - lax.rem(k, 2)
    x = lax.rem(r // 4 + dx, 4)
    y = lax.rem(lax.rem(c, 2) * 2 + lax.rem(r // 2, 2) + dy, 4)
    core = lax.rem(r + dk, 2)
    return x * 4 + lax.rem(y, 2) * 2 + core, (c // 2) * 2 + y // 2


def depth_peer(k):
    r, c = spot()
    z = lax.rem(c // 2 + far_first(k, 8), 16)
    return r, z * 2 + lax.rem(c, 2)


AROUND = [(-1, 0), (1, 0), (0, -1), (0, 1), (-1, -1), (-1, 1), (1, -1), (1, 1)]


def each(count, body):
    def step(k, carry):
        body(k)
        return carry

    lax.fori_loop(0, count, step, 0)


def along(dz):
    r, c = spot()
    return r, lax.rem(c // 2 + 16 + dz, 16) * 2 + lax.rem(c, 2)


def tell(semaphore, device):
    pl.semaphore_signal(semaphore, inc=1, device_id=device, device_id_type=MESH)


def enter():
    barrier = pltpu.get_barrier_semaphore()
    for dr, dc in AROUND:
        tell(barrier, beside(dr, dc))
    each(31, lambda k: tell(barrier, plane_peer(k)))
    for dz in (1, -1):
        tell(barrier, along(dz))


def entered():
    pl.semaphore_wait(pltpu.get_barrier_semaphore(), 8 + 31 + 2)


def dot(a, b):
    return jnp.dot(a, b, preferred_element_type=F32)


def gate(v):
    return v * jnp.minimum(jnp.maximum(v + 3.0, 0.0), 6.0)


def inside(rows, halo, lanes):
    r, c = spot()
    at = lax.broadcasted_iota(jnp.int32, (rows * PITCH, lanes), 0)
    row = at // PITCH
    col = at - row * PITCH
    row = row + (r * ROWS - halo)
    col = col + (c * COLS - halo)
    ok = (row >= 0) & (row < 128) & (col >= 0) & (col < 1024)
    return jnp.where(ok, 1.0, 0.0).astype(F32)


def pack(tile, left, right, packed, wide):
    for r in range(ROWS):
        row = tile(r)
        packed[0, 4 * r : 4 * r + 4, :wide] = row[0:4]
        packed[1, 4 * r : 4 * r + 4, :wide] = row[COLS - 4 : COLS]
    left[...] = packed[0, :, :wide].astype(BF16)
    right[...] = packed[1, :, :wide].astype(BF16)


def trade(tile, left, right, halo, across, sides, corners, send, recv):
    low = tile.at[pl.ds(ROWS - halo, halo)]
    high = tile.at[pl.ds(0, halo)]
    top = pl.ds(0, 16)
    bottom = pl.ds(16, 16)
    plan = [
        ((1, 0), low, across.at[0]),
        ((-1, 0), high, across.at[1]),
        ((0, 1), right, sides.at[0]),
        ((0, -1), left, sides.at[1]),
        ((1, 1), right.at[bottom], corners.at[0]),
        ((1, -1), left.at[bottom], corners.at[1]),
        ((-1, 1), right.at[top], corners.at[2]),
        ((-1, -1), left.at[top], corners.at[3]),
    ]
    return [
        pltpu.make_async_remote_copy(
            src_ref=src,
            dst_ref=dst,
            send_sem=send.at[i],
            recv_sem=recv.at[i],
            device_id=beside(*where),
            device_id_type=MESH,
        )
        for i, (where, src, dst) in enumerate(plan)
    ]


def assemble(out, tile, halo, across, sides, corners):
    wide = out.shape[1]
    skip = 4 - halo
    ends = halo + COLS

    def put(row, col, value):
        start = row * PITCH + col
        out[start : start + value.shape[0], :] = value

    for r in range(ROWS):
        put(halo + r, halo, tile[r].astype(F32))
    for r in range(halo):
        put(r, halo, across[0, r].astype(F32))
        put(halo + ROWS + r, halo, across[1, r].astype(F32))
    west = sides[0].astype(F32)
    east = sides[1].astype(F32)
    for r in range(ROWS):
        put(halo + r, 0, west[4 * r + skip : 4 * r + 4])
        put(halo + r, ends, east[4 * r : 4 * r + halo])
    nw, ne, sw, se = [corners[i].astype(F32) for i in range(4)]
    for r in range(halo):
        low = 4 * (r + skip)
        put(r, 0, nw[low + skip : low + 4])
        put(r, ends, ne[low : low + halo])
        put(halo + ROWS + r, 0, sw[4 * r + skip : 4 * r + 4])
        put(halo + ROWS + r, ends, se[4 * r : 4 * r + halo])


def prepare(qkv_weight, agg_depth, agg_group, qkv_w, agg_w, grp_w, stack):
    i = lax.broadcasted_iota(jnp.int32, (3 * WIDTH, 3 * WIDTH), 0)
    j = lax.broadcasted_iota(jnp.int32, (3 * WIDTH, 3 * WIDTH), 1)
    kind = j // WIDTH
    head = (j - kind * WIDTH) // HD
    lane = j - (j // HD) * HD
    order = jnp.where(i == head * (3 * HD) + kind * HD + lane, 1.0, 0.0).astype(BF16)
    stack[...] = jnp.zeros_like(stack)
    for s in range(2):
        qkv_w[s] = dot(qkv_weight[s], order).astype(BF16)
        for a in range(5):
            for b in range(5):
                at = 40 * s + 8 * a + b
                stack[at : at + 1] = agg_depth[a, b, s : s + 1]
    full = stack[...]
    high = full.astype(BF16)
    rest = full - high.astype(F32)
    mid = rest.astype(BF16)
    low = (rest - mid.astype(F32)).astype(BF16)
    moved = dot(high, order) + dot(mid, order) + dot(low, order)
    i = lax.broadcasted_iota(jnp.int32, (HD, WIDTH), 0)
    j = lax.broadcasted_iota(jnp.int32, (HD, WIDTH), 1)
    spread = jnp.where(i == j - (j // HD) * HD, 1.0, 0.0).astype(BF16)
    i = lax.broadcasted_iota(jnp.int32, (WIDTH, WIDTH), 0)
    j = lax.broadcasted_iota(jnp.int32, (WIDTH, WIDTH), 1)
    same = i // HD == j // HD
    for s in range(2):
        agg_w[s] = moved[40 * s : 40 * s + 40]
        for t in range(3):
            rows = jnp.concatenate([agg_group[s, 3 * h + t] for h in range(HEADS)], axis=0)
            grp_w[s, t] = jnp.where(same, dot(rows, spread), 0.0).astype(BF16)


def kernel(*refs):
    given, (out_map, out_boxes), held = refs[:14], refs[14:16], refs[16:30]
    (
        features,
        expand_weight,
        expand_bias,
        depth_weight,
        depth_bias,
        project_weight,
        project_bias,
        qkv_weight,
        agg_depth,
        agg_group,
        output_weight,
        output_bias,
        head_weight,
        head_bias,
    ) = held
    (
        xp,
        xb,
        edge3,
        edge2,
        hidden,
        spread,
        acc,
        qkv,
        scaled,
        center,
        mixed,
        joined,
        qkv_w,
        agg_w,
        grp_w,
        stack,
        head_w,
        packed,
        lefts,
        rights,
        f_left,
        f_right,
        tile,
        f_across,
        f_sides,
        f_corners,
        across3,
        across1,
        sides,
        corners,
        part,
        got,
        mine,
        deep,
        total,
        whole,
        table,
        keys,
        hs_send,
        hs_recv,
        ar_send,
        ar_recv,
        ring,
        load,
    ) = refs[30:]
    loads = [
        pltpu.make_async_copy(src, dst, load.at[i]) for i, (src, dst) in enumerate(zip(given, held))
    ]
    for copy in loads:
        copy.start()
    enter()
    xp[...] = jnp.zeros_like(xp)
    joined[...] = jnp.zeros_like(joined)
    part[...] = jnp.zeros_like(part)
    head_w[...] = jnp.zeros_like(head_w)
    edge3[...] = inside(14, 3, 128) * (1.0 / 6.0)
    edge2[...] = inside(12, 2, 128)
    loads[0].wait()
    pack(lambda r: features[r].astype(F32), f_left, f_right, packed, WIDTH)
    entered()
    first = trade(
        features, f_left, f_right, 3, f_across, f_sides, f_corners, hs_send.at[2], hs_recv.at[2]
    )
    for copy in first:
        copy.start()
    for dz in (1, -1):
        tell(ring.at[0], along(dz))
    for copy in loads[1:]:
        copy.wait()
    prepare(qkv_weight, agg_depth, agg_group, qkv_w, agg_w, grp_w, stack)
    for a in range(3):
        for b in range(3):
            at = 8 * (3 * a + b)
            head_w[at : at + 4] = head_weight[a, b].astype(F32)
    pl.semaphore_wait(ring.at[0], 2)
    for dz in (2, -2):
        tell(ring.at[1], along(dz))
    for copy in first:
        copy.wait()
    assemble(xp, features, 3, f_across, f_sides, f_corners)
    xb[...] = xp[...].astype(BF16)

    for s in range(2):
        halo = HALOS[s]
        acc[...] = jnp.zeros_like(acc)

        def expand(c, carry, s=s):
            wide = pl.ds(pl.multiple_of(c * CHUNK, CHUNK), CHUNK)
            value = gate(dot(xb[...], expand_weight[s, :, wide]) + expand_bias[s : s + 1, wide])
            for l in range(CHUNK // 128):
                hidden[:, 128 * l : 128 * l + 128] = (
                    value[:, 128 * l : 128 * l + 128] * edge3[...]
                )
            for l in range(CHUNK // 128):
                here = slice(128 * l, 128 * l + 128)
                lanes = pl.ds(pl.multiple_of(c * CHUNK + 128 * l, 128), 128)
                taps = [
                    [depth_weight[a, b, s : s + 1, lanes] for b in range(3)] for a in range(3)
                ]
                bias = depth_bias[s : s + 1, lanes]
                for pair in range(6):
                    done = []
                    for r in (2 * pair, 2 * pair + 1):
                        rows = [
                            hidden[PITCH * (r + a) : PITCH * (r + a) + PITCH, here]
                            for a in range(3)
                        ]
                        cols = [
                            rows[0] * taps[0][b] + rows[1] * taps[1][b] + rows[2] * taps[2][b]
                            for b in range(3)
                        ]
                        value = (
                            cols[0]
                            + pltpu.roll(cols[1], PITCH - 1, 0)
                            + pltpu.roll(cols[2], PITCH - 2, 0)
                            + bias
                        )
                        done.append(gate(value) * (1.0 / 6.0))
                    spread[2 * PITCH * pair : 2 * PITCH * (pair + 1), here] = jnp.concatenate(
                        done, axis=0
                    ).astype(BF16)
            acc[...] += dot(spread[...], project_weight[s, wide, :])
            return carry

        lax.fori_loop(0, EXPANDED // CHUNK, expand, 0)
        if s == 0:
            pl.semaphore_wait(ring.at[1], 2)
            for dz in (4, -4):
                tell(ring.at[2], along(dz))
        bias = project_bias[s : s + 1]
        for r in range(12):
            here = slice(PITCH * r, PITCH * r + PITCH)
            base = xp[PITCH * (r + 1) : PITCH * (r + 2)]
            value = acc[here] + pltpu.roll(base, PITCH - 1, 0) + bias
            for l in range(WIDTH // 128):
                lanes = slice(128 * l, 128 * l + 128)
                mixed[here, lanes] = value[:, lanes] * edge2[here]
        qkv[...] = dot(mixed[...].astype(BF16), qkv_w[s])

        def taps5(l, carry, s=s):
            lanes = pl.ds(pl.multiple_of(l * 128, 128), 128)
            for r in range(ROWS):
                cols = [None] * 5
                for a in range(5):
                    row = qkv[PITCH * (r + a) : PITCH * (r + a) + PITCH, lanes]
                    for b in range(5):
                        term = row * agg_w[s, 8 * a + b : 8 * a + b + 1, lanes]
                        cols[b] = term if a == 0 else cols[b] + term
                value = cols[0]
                for b in range(1, 5):
                    value = value + pltpu.roll(cols[b], PITCH - b, 0)
                scaled[COLS * r : COLS * r + COLS, lanes] = value[0:COLS].astype(BF16)
                near = pltpu.roll(qkv[PITCH * (r + 2) : PITCH * (r + 3), lanes], PITCH - 2, 0)
                center[COLS * r : COLS * r + COLS, lanes] = near[0:COLS].astype(BF16)
            return carry

        def kind(t):
            lanes = slice(WIDTH * t, WIDTH * t + WIDTH)
            return [center[:, lanes], dot(scaled[:, lanes], grp_w[s, t]).astype(BF16)]

        lax.fori_loop(2, 6, taps5, 0)
        lane = lax.broadcasted_iota(jnp.int32, (HD, 128), 1) // HD
        ones = jnp.ones((16, ROWS * COLS), BF16)
        for branch, (k, v) in enumerate(zip(kind(1), kind(2))):
            k = jnp.maximum(k, jnp.zeros_like(k))
            outer = lax.dot_general(k, v, (((0,), (0,)), ((), ())), preferred_element_type=F32)
            count = dot(ones, k)
            for g in range(2):
                group = 2 * branch + g
                lanes = slice(128 * g, 128 * g + 128)
                fold = jnp.zeros((HD, 128), F32)
                for h in range(4):
                    low = 128 * g + HD * h
                    fold = jnp.where(lane == h, outer[low : low + HD, lanes], fold)
                for p in range(8):
                    part[s, 8 * group + p, 0:4, :] = fold[4 * p : 4 * p + 4]
                part[s, group, 4:5, :] = count[0:1, lanes]

        me = plane_of(*spot())
        depth = spot()[1] // 2

        def remote(src, dst, stage, device):
            return pltpu.make_async_remote_copy(
                src_ref=src,
                dst_ref=dst,
                send_sem=ar_send.at[s, stage],
                recv_sem=ar_recv.at[s, stage],
                device_id=device,
                device_id_type=MESH,
            )

        def send1(k, s=s):
            device = plane_peer(k)
            remote(part.at[s, plane_of(*device)], got.at[s, me], 0, device).start()

        def send2(k, s=s):
            remote(mine.at[s], deep.at[s, depth], 1, depth_peer(k)).start()

        def send3(k, s=s):
            remote(total.at[s], whole.at[s, me], 2, plane_peer(k)).start()

        def arrived(buffer, count, stage, s=s):
            view = buffer.at[s, pl.ds(0, count)]
            pltpu.make_async_copy(view, view, ar_recv.at[s, stage]).wait()

        def sent(buffer, count, stage, s=s):
            view = buffer.at[s, pl.ds(0, count)]
            pltpu.make_async_copy(view, view, ar_send.at[s, stage]).wait()

        each(31, send1)
        got[s, me] = part[s, me]

        lax.fori_loop(0, 2, taps5, 0)
        near, far = kind(0)
        for r in range(ROWS):
            here = slice(COLS * r, COLS * r + COLS)
            value = pltpu.roll(mixed[PITCH * (r + 2) : PITCH * (r + 3)], PITCH - 2, 0)
            tile[s, r, :, 0:WIDTH] = value[0:COLS].astype(BF16)
            tile[s, r, :, WIDTH : 2 * WIDTH] = jnp.maximum(near[here], jnp.zeros_like(near[here]))
            tile[s, r, :, 2 * WIDTH :] = jnp.maximum(far[here], jnp.zeros_like(far[here]))
        pack(
            lambda r, s=s: tile[s, r].astype(F32), lefts.at[s], rights.at[s], packed, 3 * WIDTH
        )
        across = across3 if halo == 3 else across1
        swap = trade(
            tile.at[s],
            lefts.at[s],
            rights.at[s],
            halo,
            across,
            sides.at[s],
            corners.at[s],
            hs_send.at[s],
            hs_recv.at[s],
        )

        arrived(got, 31, 0)
        mine[s] = jnp.sum(got[s], axis=0)
        if s == 0:
            pl.semaphore_wait(ring.at[2], 2)
        each(15, send2)
        deep[s, depth] = mine[s]
        for copy in swap:
            copy.start()
        for copy in swap:
            copy.wait()
        area = (ROWS + 2 * halo) * PITCH
        assemble(joined.at[pl.ds(0, area)], tile.at[s], halo, across, sides.at[s], corners.at[s])
        arrived(deep, 15, 1)
        total[s] = jnp.sum(deep[s], axis=0)
        each(31, send3)
        whole[s, me] = total[s]
        arrived(whole, 31, 2)
        sent(got, 31, 0)
        sent(deep, 15, 1)
        sent(whole, 31, 2)

        for p in range(32):
            table[4 * p : 4 * p + 4, :] = whole[s, p, 0:4, :]
        i = lax.broadcasted_iota(jnp.int32, (WIDTH, WIDTH), 0)
        j = lax.broadcasted_iota(jnp.int32, (WIDTH, WIDTH), 1)
        same = i // HD == j // HD
        ones = jnp.where(same, 1.0, 0.0).astype(BF16)
        attended = []
        for branch in range(2):
            blocks = []
            for g in range(2):
                group = 2 * branch + g
                block = table[HD * group : HD * group + HD]
                blocks.append(jnp.concatenate([block] * 4, axis=0))
                keys[0:1, 128 * g : 128 * g + 128] = whole[s, group, 4:5, :]
            numer_w = jnp.where(
                same, jnp.concatenate([jnp.concatenate([b, b], axis=1) for b in blocks], axis=0), 0.0
            )
            key_row = jnp.broadcast_to(keys[0:1, :], (WIDTH, WIDTH))
            denom_w = dot(jnp.where(i == j, key_row, 0.0).astype(BF16), ones)
            q = joined[0:area, WIDTH * (1 + branch) : WIDTH * (2 + branch)].astype(BF16)
            numer = dot(q, numer_w.astype(BF16))
            denom = dot(q, denom_w.astype(BF16))
            attended.append((numer / (denom + 1e-06)).astype(BF16))
        value = (
            joined[0:area, 0:WIDTH]
            + dot(attended[0], output_weight[s, 0:WIDTH])
            + dot(attended[1], output_weight[s, WIDTH:])
            + output_bias[s : s + 1]
        )
        xp[0:area] = value
        xb[0:area] = value.astype(BF16)

    for r in range(ROWS):
        start = PITCH * (r + 1) + 1
        out_map[r] = xp[start : start + COLS].astype(BF16)
    area = 10 * PITCH
    on_map = inside(10, 1, 128)
    final = jnp.concatenate(
        [
            (xp[0:area, 128 * l : 128 * l + 128] * on_map).astype(BF16)
            for l in range(WIDTH // 128)
        ],
        axis=1,
    )
    final = jnp.concatenate([final, jnp.zeros((512 - area, WIDTH), BF16)], axis=0)
    taps = lax.dot_general(
        head_w[...].astype(BF16), final, (((1,), (1,)), ((), ())), preferred_element_type=F32
    )
    boxes = jnp.zeros((8, 512), F32)
    for a in range(3):
        for b in range(3):
            at = 8 * (3 * a + b)
            shift = PITCH * a + b
            term = taps[at : at + 8]
            boxes = boxes + (term if shift == 0 else pltpu.roll(term, 512 - shift, 1))
    for r in range(ROWS):
        row = boxes if r == 0 else pltpu.roll(boxes, 512 - PITCH * r, 1)
        for o in range(4):
            out_boxes[o, r : r + 1, :] = row[o : o + 1, 0:COLS] + head_bias[o]


def local(*args):
    args = list(args)
    for i in (3, 8):
        args[i] = jnp.transpose(args[i], (1, 2, 0, 3))
    dma = pltpu.SemaphoreType.DMA
    vmem = pltpu.VMEM
    area = 14 * PITCH
    inner = 12 * PITCH
    wide = 3 * WIDTH
    held = [vmem(a.shape, a.dtype) for a in args[:13]] + [pltpu.SMEM((4,), F32)]
    scratch = held + [
        vmem((area, WIDTH), F32),
        vmem((area, WIDTH), BF16),
        vmem((area, 128), F32),
        vmem((inner, 128), F32),
        vmem((area, CHUNK), F32),
        vmem((inner, CHUNK), BF16),
        vmem((inner, WIDTH), F32),
        vmem((inner, wide), F32),
        vmem((ROWS * COLS, wide), BF16),
        vmem((ROWS * COLS, wide), BF16),
        vmem((inner, WIDTH), F32),
        vmem((area, wide), F32),
        vmem((2, WIDTH, wide), BF16),
        vmem((2, 40, wide), F32),
        vmem((2, 3, WIDTH, WIDTH), BF16),
        vmem((80, wide), F32),
        vmem((72, WIDTH), F32),
        vmem((2, 32, wide), F32),
        vmem((2, 32, wide), BF16),
        vmem((2, 32, wide), BF16),
        vmem((32, WIDTH), BF16),
        vmem((32, WIDTH), BF16),
        vmem((2, ROWS, COLS, wide), BF16),
        vmem((2, 3, COLS, WIDTH), BF16),
        vmem((2, 32, WIDTH), BF16),
        vmem((4, 16, WIDTH), BF16),
        vmem((2, 3, COLS, wide), BF16),
        vmem((2, 1, COLS, wide), BF16),
        vmem((2, 2, 32, wide), BF16),
        vmem((2, 4, 16, wide), BF16),
        vmem((2, 32, 5, 128), F32),
        vmem((2, 32, 5, 128), F32),
        vmem((2, 5, 128), F32),
        vmem((2, 16, 5, 128), F32),
        vmem((2, 5, 128), F32),
        vmem((2, 32, 5, 128), F32),
        vmem((128, 128), F32),
        vmem((8, WIDTH), F32),
        dma((3, 8)),
        dma((3, 8)),
        dma((2, 3)),
        dma((2, 3)),
        pltpu.SemaphoreType.REGULAR((3,)),
        dma((14,)),
    ]
    in_vmem = pl.BlockSpec(memory_space=pltpu.VMEM)
    return pl.pallas_call(
        kernel,
        out_shape=(
            jax.ShapeDtypeStruct((ROWS, COLS, WIDTH), BF16),
            jax.ShapeDtypeStruct((4, ROWS, COLS), F32),
        ),
        in_specs=[pl.BlockSpec(memory_space=pl.ANY)] * 14,
        out_specs=(in_vmem, in_vmem),
        scratch_shapes=scratch,
        compiler_params=pltpu.CompilerParams(
            collective_id=0, has_side_effects=True, vmem_limit_bytes=60 * 1024 * 1024
        ),
    )(*args)


def solution(mesh):
    return jax.shard_map(
        local,
        mesh=mesh,
        in_specs=(P("row", "col", None),) + (P(),) * 13,
        out_specs=(P("row", "col", None), P(None, "row", "col")),
        check_vma=False,
    )
```

```python
import functools

import jax
import jax.numpy as jnp
from jax import lax
from jax.experimental import pallas as pl
from jax.experimental.pallas import tpu as pltpu
from jax.sharding import PartitionSpec as P

MESH = pl.DeviceIdType.MESH
F32 = jnp.float32
BF16 = jnp.bfloat16
ROWS = 8
COLS = 32
PITCH = 40
WIDTH = 256
EXPANDED = 1024
CHUNK = 256
HD = 32
HEADS = 8
HALOS = (3, 1)


def spot():
    return lax.axis_index("row"), lax.axis_index("col")


def beside(dr, dc):
    r, c = spot()
    return lax.rem(r + 16 + dr, 16), lax.rem(c + 32 + dc, 32)


def plane_of(r, c):
    return r * 2 + lax.rem(c, 2)


def hops(step, around):
    return min(step, around - step)


PLANE = sorted(
    [(x, y, k) for x in range(4) for y in range(4) for k in range(2) if x or y or k],
    key=lambda step: -hops(step[0], 4) - hops(step[1], 4),
)
DEPTH = sorted(range(1, 16), key=lambda step: -hops(step, 16))


def plane_peers():
    r, c = spot()
    y = lax.rem(c, 2) * 2 + lax.rem(r // 2, 2)
    k = lax.rem(r, 2)
    first = [lax.rem(r // 4 + step, 4) * 4 for step in range(4)]
    ys = [lax.rem(y + step, 4) for step in range(4)]
    second = [lax.rem(at, 2) * 2 for at in ys]
    cols = [(c // 2) * 2 + at // 2 for at in ys]
    cores = [k, 1 - k]
    return [(first[x] + second[y] + cores[k], cols[y]) for x, y, k in PLANE]


def depth_peers():
    return [along(step) for step in DEPTH]


AROUND = [(-1, 0), (1, 0), (0, -1), (0, 1), (-1, -1), (-1, 1), (1, -1), (1, 1)]


def each(count, body):
    def step(k, carry):
        body(k)
        return carry

    lax.fori_loop(0, count, step, 0)


def along(dz):
    r, c = spot()
    return r, lax.rem(c // 2 + 16 + dz, 16) * 2 + lax.rem(c, 2)


def tell(semaphore, device):
    pl.semaphore_signal(semaphore, inc=1, device_id=device, device_id_type=MESH)


def enter():
    barrier = pltpu.get_barrier_semaphore()
    for dr, dc in AROUND:
        tell(barrier, beside(dr, dc))
    for device in plane_peers():
        tell(barrier, device)
    for dz in (1, -1):
        tell(barrier, along(dz))


def entered():
    pl.semaphore_wait(pltpu.get_barrier_semaphore(), 8 + 31 + 2)


def dot(a, b):
    return jnp.dot(a, b, preferred_element_type=F32)


def gate(v):
    return v * jnp.minimum(jnp.maximum(v + 3.0, 0.0), 6.0)


def inside(rows, halo, lanes):
    r, c = spot()
    at = lax.broadcasted_iota(jnp.int32, (rows * PITCH, lanes), 0)
    row = at // PITCH
    col = at - row * PITCH
    row = row + (r * ROWS - halo)
    col = col + (c * COLS - halo)
    ok = (row >= 0) & (row < 128) & (col >= 0) & (col < 1024)
    return jnp.where(ok, 1.0, 0.0).astype(F32)


def pack(tile, left, right, packed, wide):
    for r in range(ROWS):
        row = tile(r)
        packed[0, 4 * r : 4 * r + 4, :wide] = row[0:4]
        packed[1, 4 * r : 4 * r + 4, :wide] = row[COLS - 4 : COLS]
    left[...] = packed[0, :, :wide].astype(BF16)
    right[...] = packed[1, :, :wide].astype(BF16)


def trade(tile, left, right, halo, across, sides, corners, send, recv):
    low = tile.at[pl.ds(ROWS - halo, halo)]
    high = tile.at[pl.ds(0, halo)]
    top = pl.ds(0, 16)
    bottom = pl.ds(16, 16)
    plan = [
        ((1, 0), low, across.at[0]),
        ((-1, 0), high, across.at[1]),
        ((0, 1), right, sides.at[0]),
        ((0, -1), left, sides.at[1]),
        ((1, 1), right.at[bottom], corners.at[0]),
        ((1, -1), left.at[bottom], corners.at[1]),
        ((-1, 1), right.at[top], corners.at[2]),
        ((-1, -1), left.at[top], corners.at[3]),
    ]
    return [
        pltpu.make_async_remote_copy(
            src_ref=src,
            dst_ref=dst,
            send_sem=send.at[i],
            recv_sem=recv.at[i],
            device_id=beside(*where),
            device_id_type=MESH,
        )
        for i, (where, src, dst) in enumerate(plan)
    ]


def assemble(out, tile, halo, across, sides, corners):
    wide = out.shape[1]
    skip = 4 - halo
    ends = halo + COLS

    def put(row, col, value):
        start = row * PITCH + col
        out[start : start + value.shape[0], :] = value

    for r in range(ROWS):
        put(halo + r, halo, tile[r].astype(F32))
    for r in range(halo):
        put(r, halo, across[0, r].astype(F32))
        put(halo + ROWS + r, halo, across[1, r].astype(F32))
    west = sides[0].astype(F32)
    east = sides[1].astype(F32)
    for r in range(ROWS):
        put(halo + r, 0, west[4 * r + skip : 4 * r + 4])
        put(halo + r, ends, east[4 * r : 4 * r + halo])
    nw, ne, sw, se = [corners[i].astype(F32) for i in range(4)]
    for r in range(halo):
        low = 4 * (r + skip)
        put(r, 0, nw[low + skip : low + 4])
        put(r, ends, ne[low : low + halo])
        put(halo + ROWS + r, 0, sw[4 * r + skip : 4 * r + 4])
        put(halo + ROWS + r, ends, se[4 * r : 4 * r + halo])


def prepare(qkv_weight, agg_depth, agg_group, qkv_w, agg_w, grp_w, stack):
    i = lax.broadcasted_iota(jnp.int32, (3 * WIDTH, 3 * WIDTH), 0)
    j = lax.broadcasted_iota(jnp.int32, (3 * WIDTH, 3 * WIDTH), 1)
    kind = j // WIDTH
    head = (j - kind * WIDTH) // HD
    lane = j - (j // HD) * HD
    order = jnp.where(i == head * (3 * HD) + kind * HD + lane, 1.0, 0.0).astype(BF16)
    stack[...] = jnp.zeros_like(stack)
    for s in range(2):
        qkv_w[s] = dot(qkv_weight[s], order).astype(BF16)
        for a in range(5):
            for b in range(5):
                at = 40 * s + 8 * a + b
                stack[at : at + 1] = agg_depth[a, b, s : s + 1]
    full = stack[...]
    high = full.astype(BF16)
    rest = full - high.astype(F32)
    mid = rest.astype(BF16)
    low = (rest - mid.astype(F32)).astype(BF16)
    moved = dot(high, order) + dot(mid, order) + dot(low, order)
    i = lax.broadcasted_iota(jnp.int32, (HD, WIDTH), 0)
    j = lax.broadcasted_iota(jnp.int32, (HD, WIDTH), 1)
    spread = jnp.where(i == j - (j // HD) * HD, 1.0, 0.0).astype(BF16)
    i = lax.broadcasted_iota(jnp.int32, (WIDTH, WIDTH), 0)
    j = lax.broadcasted_iota(jnp.int32, (WIDTH, WIDTH), 1)
    same = i // HD == j // HD
    for s in range(2):
        agg_w[s] = moved[40 * s : 40 * s + 40]
        for t in range(3):
            rows = jnp.concatenate([agg_group[s, 3 * h + t] for h in range(HEADS)], axis=0)
            grp_w[s, t] = jnp.where(same, dot(rows, spread), 0.0).astype(BF16)


def kernel(*refs):
    given, (out_map, out_boxes), held = refs[:14], refs[14:16], refs[16:30]
    (
        features,
        expand_weight,
        expand_bias,
        depth_weight,
        depth_bias,
        project_weight,
        project_bias,
        qkv_weight,
        agg_depth,
        agg_group,
        output_weight,
        output_bias,
        head_weight,
        head_bias,
    ) = held
    (
        xp,
        xb,
        edge3,
        edge2,
        hidden,
        spread,
        acc,
        qkv,
        scaled,
        center,
        mixed,
        joined,
        qkv_w,
        agg_w,
        grp_w,
        stack,
        head_w,
        packed,
        lefts,
        rights,
        f_left,
        f_right,
        tile,
        f_across,
        f_sides,
        f_corners,
        across3,
        across1,
        sides,
        corners,
        part,
        got,
        mine,
        deep,
        total,
        whole,
        table,
        keys,
        hs_send,
        hs_recv,
        ar_send,
        ar_recv,
        ring,
        load,
    ) = refs[30:]
    loads = [
        pltpu.make_async_copy(src, dst, load.at[i]) for i, (src, dst) in enumerate(zip(given, held))
    ]
    for copy in loads:
        copy.start()
    enter()
    xp[...] = jnp.zeros_like(xp)
    joined[...] = jnp.zeros_like(joined)
    part[...] = jnp.zeros_like(part)
    head_w[...] = jnp.zeros_like(head_w)
    edge3[...] = inside(14, 3, 128) * (1.0 / 6.0)
    edge2[...] = inside(12, 2, 128)
    loads[0].wait()
    pack(lambda r: features[r].astype(F32), f_left, f_right, packed, WIDTH)
    entered()
    first = trade(
        features, f_left, f_right, 3, f_across, f_sides, f_corners, hs_send.at[2], hs_recv.at[2]
    )
    for copy in first:
        copy.start()
    for dz in (1, -1):
        tell(ring.at[0], along(dz))
    for copy in loads[1:]:
        copy.wait()
    prepare(qkv_weight, agg_depth, agg_group, qkv_w, agg_w, grp_w, stack)
    for a in range(3):
        for b in range(3):
            at = 8 * (3 * a + b)
            head_w[at : at + 4] = head_weight[a, b].astype(F32)
    pl.semaphore_wait(ring.at[0], 2)
    for dz in (2, -2):
        tell(ring.at[1], along(dz))
    for copy in first:
        copy.wait()
    assemble(xp, features, 3, f_across, f_sides, f_corners)
    xb[...] = xp[...].astype(BF16)

    for s in range(2):
        halo = HALOS[s]
        def grow(c, lanes, s=s):
            value = gate(dot(xb[...], expand_weight[s, :, lanes]) + expand_bias[s : s + 1, lanes])
            for l in range(CHUNK // 128):
                hidden[c, :, 128 * l : 128 * l + 128] = (
                    value[:, 128 * l : 128 * l + 128] * edge3[...]
                )

        def filter3(source, lanes, s=s):
            taps = [[depth_weight[a, b, s : s + 1, lanes] for b in range(3)] for a in range(3)]
            bias = depth_bias[s : s + 1, lanes]
            for pair in range(6):
                done = []
                for r in (2 * pair, 2 * pair + 1):
                    rows = [source(PITCH * (r + a)) for a in range(3)]
                    cols = [
                        rows[0] * taps[0][b] + rows[1] * taps[1][b] + rows[2] * taps[2][b]
                        for b in range(3)
                    ]
                    value = (
                        cols[0]
                        + pltpu.roll(cols[1], PITCH - 1, 0)
                        + pltpu.roll(cols[2], PITCH - 2, 0)
                        + bias
                    )
                    done.append(gate(value))
                spread[2 * PITCH * pair : 2 * PITCH * (pair + 1), lanes] = jnp.concatenate(
                    done, axis=0
                ).astype(BF16)

        for c in range(EXPANDED // CHUNK):
            grow(c, slice(c * CHUNK, c * CHUNK + CHUNK))
            for l in range(CHUNK // 128):
                filter3(
                    lambda at, c=c, l=l: hidden[c, at : at + PITCH, 128 * l : 128 * l + 128],
                    slice(c * CHUNK + 128 * l, c * CHUNK + 128 * l + 128),
                )
        acc[...] = dot(spread[...], project_weight[s]) * (1.0 / 6.0)
        if s == 0:
            pl.semaphore_wait(ring.at[1], 2)
            for dz in (4, -4):
                tell(ring.at[2], along(dz))
        bias = project_bias[s : s + 1]
        for r in range(12):
            here = slice(PITCH * r, PITCH * r + PITCH)
            base = xp[PITCH * (r + 1) : PITCH * (r + 2)]
            value = acc[here] + pltpu.roll(base, PITCH - 1, 0) + bias
            for l in range(WIDTH // 128):
                lanes = slice(128 * l, 128 * l + 128)
                mixed[here, lanes] = value[:, lanes] * edge2[here]
        qkv[...] = dot(mixed[...].astype(BF16), qkv_w[s])

        def taps5(l, carry, s=s):
            lanes = pl.ds(pl.multiple_of(l * 128, 128), 128)
            for r in range(ROWS):
                cols = [None] * 5
                for a in range(5):
                    row = qkv[PITCH * (r + a) : PITCH * (r + a) + PITCH, lanes]
                    for b in range(5):
                        term = row * agg_w[s, 8 * a + b : 8 * a + b + 1, lanes]
                        cols[b] = term if a == 0 else cols[b] + term
                value = cols[0]
                for b in range(1, 5):
                    value = value + pltpu.roll(cols[b], PITCH - b, 0)
                scaled[COLS * r : COLS * r + COLS, lanes] = value[0:COLS].astype(BF16)
                near = pltpu.roll(qkv[PITCH * (r + 2) : PITCH * (r + 3), lanes], PITCH - 2, 0)
                center[COLS * r : COLS * r + COLS, lanes] = near[0:COLS].astype(BF16)
            return carry

        def kind(t):
            lanes = slice(WIDTH * t, WIDTH * t + WIDTH)
            return [center[:, lanes], dot(scaled[:, lanes], grp_w[s, t]).astype(BF16)]

        lax.fori_loop(2, 6, taps5, 0)
        lane = lax.broadcasted_iota(jnp.int32, (HD, 128), 1) // HD
        ones = jnp.ones((16, ROWS * COLS), BF16)
        for branch, (k, v) in enumerate(zip(kind(1), kind(2))):
            k = jnp.maximum(k, jnp.zeros_like(k))
            outer = lax.dot_general(k, v, (((0,), (0,)), ((), ())), preferred_element_type=F32)
            count = dot(ones, k)
            for g in range(2):
                group = 2 * branch + g
                lanes = slice(128 * g, 128 * g + 128)
                fold = jnp.zeros((HD, 128), F32)
                for h in range(4):
                    low = 128 * g + HD * h
                    fold = jnp.where(lane == h, outer[low : low + HD, lanes], fold)
                for p in range(8):
                    part[s, 8 * group + p, 0:4, :] = fold[4 * p : 4 * p + 4]
                part[s, group, 4:5, :] = count[0:1, lanes]

        me = plane_of(*spot())
        depth = spot()[1] // 2

        def remote(src, dst, stage, device):
            return pltpu.make_async_remote_copy(
                src_ref=src,
                dst_ref=dst,
                send_sem=ar_send.at[s, stage],
                recv_sem=ar_recv.at[s, stage],
                device_id=device,
                device_id_type=MESH,
            )

        def arrived(buffer, count, stage, s=s):
            view = buffer.at[s, pl.ds(0, count)]
            pltpu.make_async_copy(view, view, ar_recv.at[s, stage]).wait()

        def sent(buffer, count, stage, s=s):
            view = buffer.at[s, pl.ds(0, count)]
            pltpu.make_async_copy(view, view, ar_send.at[s, stage]).wait()

        for device in plane_peers():
            remote(part.at[s, plane_of(*device)], got.at[s, me], 0, device).start()
        got[s, me] = part[s, me]

        lax.fori_loop(0, 2, taps5, 0)
        near, far = kind(0)
        for r in range(ROWS):
            here = slice(COLS * r, COLS * r + COLS)
            value = pltpu.roll(mixed[PITCH * (r + 2) : PITCH * (r + 3)], PITCH - 2, 0)
            tile[s, r, :, 0:WIDTH] = value[0:COLS].astype(BF16)
            tile[s, r, :, WIDTH : 2 * WIDTH] = jnp.maximum(near[here], jnp.zeros_like(near[here]))
            tile[s, r, :, 2 * WIDTH :] = jnp.maximum(far[here], jnp.zeros_like(far[here]))
        pack(
            lambda r, s=s: tile[s, r].astype(F32), lefts.at[s], rights.at[s], packed, 3 * WIDTH
        )
        across = across3 if halo == 3 else across1
        swap = trade(
            tile.at[s],
            lefts.at[s],
            rights.at[s],
            halo,
            across,
            sides.at[s],
            corners.at[s],
            hs_send.at[s],
            hs_recv.at[s],
        )

        arrived(got, 31, 0)
        mine[s] = jnp.sum(got[s], axis=0)
        if s == 0:
            pl.semaphore_wait(ring.at[2], 2)
        for device in depth_peers():
            remote(mine.at[s], deep.at[s, depth], 1, device).start()
        deep[s, depth] = mine[s]
        for copy in swap:
            copy.start()
        arrived(deep, 15, 1)
        total[s] = jnp.sum(deep[s], axis=0)
        for device in plane_peers():
            remote(total.at[s], whole.at[s, me], 2, device).start()
        whole[s, me] = total[s]
        for copy in swap:
            copy.wait()
        area = (ROWS + 2 * halo) * PITCH
        assemble(joined.at[pl.ds(0, area)], tile.at[s], halo, across, sides.at[s], corners.at[s])
        arrived(whole, 31, 2)
        sent(got, 31, 0)
        sent(deep, 15, 1)
        sent(whole, 31, 2)

        for p in range(32):
            table[4 * p : 4 * p + 4, :] = whole[s, p, 0:4, :]
        i = lax.broadcasted_iota(jnp.int32, (WIDTH, WIDTH), 0)
        j = lax.broadcasted_iota(jnp.int32, (WIDTH, WIDTH), 1)
        same = i // HD == j // HD
        ones = jnp.where(same, 1.0, 0.0).astype(BF16)
        attended = []
        for branch in range(2):
            blocks = []
            for g in range(2):
                group = 2 * branch + g
                block = table[HD * group : HD * group + HD]
                blocks.append(jnp.concatenate([block] * 4, axis=0))
                keys[0:1, 128 * g : 128 * g + 128] = whole[s, group, 4:5, :]
            numer_w = jnp.where(
                same, jnp.concatenate([jnp.concatenate([b, b], axis=1) for b in blocks], axis=0), 0.0
            )
            key_row = jnp.broadcast_to(keys[0:1, :], (WIDTH, WIDTH))
            denom_w = dot(jnp.where(i == j, key_row, 0.0).astype(BF16), ones)
            q = joined[0:area, WIDTH * (1 + branch) : WIDTH * (2 + branch)].astype(BF16)
            numer = dot(q, numer_w.astype(BF16))
            denom = dot(q, denom_w.astype(BF16))
            attended.append((numer / (denom + 1e-06)).astype(BF16))
        value = (
            joined[0:area, 0:WIDTH]
            + dot(attended[0], output_weight[s, 0:WIDTH])
            + dot(attended[1], output_weight[s, WIDTH:])
            + output_bias[s : s + 1]
        )
        xp[0:area] = value
        xb[0:area] = value.astype(BF16)

    for r in range(ROWS):
        start = PITCH * (r + 1) + 1
        out_map[r] = xp[start : start + COLS].astype(BF16)
    area = 10 * PITCH
    on_map = inside(10, 1, 128)
    final = jnp.concatenate(
        [
            (xp[0:area, 128 * l : 128 * l + 128] * on_map).astype(BF16)
            for l in range(WIDTH // 128)
        ],
        axis=1,
    )
    final = jnp.concatenate([final, jnp.zeros((512 - area, WIDTH), BF16)], axis=0)
    taps = lax.dot_general(
        head_w[...].astype(BF16), final, (((1,), (1,)), ((), ())), preferred_element_type=F32
    )
    boxes = jnp.zeros((8, 512), F32)
    for a in range(3):
        for b in range(3):
            at = 8 * (3 * a + b)
            shift = PITCH * a + b
            term = taps[at : at + 8]
            boxes = boxes + (term if shift == 0 else pltpu.roll(term, 512 - shift, 1))
    for r in range(ROWS):
        row = boxes if r == 0 else pltpu.roll(boxes, 512 - PITCH * r, 1)
        for o in range(4):
            out_boxes[o, r : r + 1, :] = row[o : o + 1, 0:COLS] + head_bias[o]


def local(*args):
    args = list(args)
    for i in (3, 8):
        args[i] = jnp.transpose(args[i], (1, 2, 0, 3))
    dma = pltpu.SemaphoreType.DMA
    vmem = pltpu.VMEM
    area = 14 * PITCH
    inner = 12 * PITCH
    wide = 3 * WIDTH
    held = [vmem(a.shape, a.dtype) for a in args[:13]] + [pltpu.SMEM((4,), F32)]
    scratch = held + [
        vmem((area, WIDTH), F32),
        vmem((area, WIDTH), BF16),
        vmem((area, 128), F32),
        vmem((inner, 128), F32),
        vmem((EXPANDED // CHUNK, area, CHUNK), F32),
        vmem((inner, EXPANDED), BF16),
        vmem((inner, WIDTH), F32),
        vmem((inner, wide), F32),
        vmem((ROWS * COLS, wide), BF16),
        vmem((ROWS * COLS, wide), BF16),
        vmem((inner, WIDTH), F32),
        vmem((area, wide), F32),
        vmem((2, WIDTH, wide), BF16),
        vmem((2, 40, wide), F32),
        vmem((2, 3, WIDTH, WIDTH), BF16),
        vmem((80, wide), F32),
        vmem((72, WIDTH), F32),
        vmem((2, 32, wide), F32),
        vmem((2, 32, wide), BF16),
        vmem((2, 32, wide), BF16),
        vmem((32, WIDTH), BF16),
        vmem((32, WIDTH), BF16),
        vmem((2, ROWS, COLS, wide), BF16),
        vmem((2, 3, COLS, WIDTH), BF16),
        vmem((2, 32, WIDTH), BF16),
        vmem((4, 16, WIDTH), BF16),
        vmem((2, 3, COLS, wide), BF16),
        vmem((2, 1, COLS, wide), BF16),
        vmem((2, 2, 32, wide), BF16),
        vmem((2, 4, 16, wide), BF16),
        vmem((2, 32, 5, 128), F32),
        vmem((2, 32, 5, 128), F32),
        vmem((2, 5, 128), F32),
        vmem((2, 16, 5, 128), F32),
        vmem((2, 5, 128), F32),
        vmem((2, 32, 5, 128), F32),
        vmem((128, 128), F32),
        vmem((8, WIDTH), F32),
        dma((3, 8)),
        dma((3, 8)),
        dma((2, 3)),
        dma((2, 3)),
        pltpu.SemaphoreType.REGULAR((3,)),
        dma((14,)),
    ]
    in_vmem = pl.BlockSpec(memory_space=pltpu.VMEM)
    return pl.pallas_call(
        kernel,
        out_shape=(
            jax.ShapeDtypeStruct((ROWS, COLS, WIDTH), BF16),
            jax.ShapeDtypeStruct((4, ROWS, COLS), F32),
        ),
        in_specs=[pl.BlockSpec(memory_space=pl.ANY)] * 14,
        out_specs=(in_vmem, in_vmem),
        scratch_shapes=scratch,
        compiler_params=pltpu.CompilerParams(
            collective_id=0, has_side_effects=True, vmem_limit_bytes=60 * 1024 * 1024
        ),
    )(*args)


def solution(mesh):
    return jax.shard_map(
        local,
        mesh=mesh,
        in_specs=(P("row", "col", None),) + (P(),) * 13,
        out_specs=(P("row", "col", None), P(None, "row", "col")),
        check_vma=False,
    )
```

```python
import functools

import jax
import jax.numpy as jnp
from jax import lax
from jax.experimental import pallas as pl
from jax.experimental.pallas import tpu as pltpu
from jax.sharding import PartitionSpec as P

MESH = pl.DeviceIdType.MESH
F32 = jnp.float32
BF16 = jnp.bfloat16
ROWS = 8
COLS = 32
PITCH = 40
WIDTH = 256
EXPANDED = 1024
CHUNK = 256
HD = 32
HEADS = 8
HALOS = (3, 1)


def spot():
    return lax.axis_index("row"), lax.axis_index("col")


def beside(dr, dc):
    r, c = spot()
    return lax.rem(r + 16 + dr, 16), lax.rem(c + 32 + dc, 32)


def plane_of(r, c):
    return r * 2 + lax.rem(c, 2)


def hops(step, around):
    return min(step, around - step)


PLANE = sorted(
    [(x, y, k) for x in range(4) for y in range(4) for k in range(2) if x or y or k],
    key=lambda step: -hops(step[0], 4) - hops(step[1], 4),
)
DEPTH = sorted(range(1, 16), key=lambda step: -hops(step, 16))


def plane_peers():
    r, c = spot()
    y = lax.rem(c, 2) * 2 + lax.rem(r // 2, 2)
    k = lax.rem(r, 2)
    first = [lax.rem(r // 4 + step, 4) * 4 for step in range(4)]
    ys = [lax.rem(y + step, 4) for step in range(4)]
    second = [lax.rem(at, 2) * 2 for at in ys]
    cols = [(c // 2) * 2 + at // 2 for at in ys]
    cores = [k, 1 - k]
    return [(first[x] + second[y] + cores[k], cols[y]) for x, y, k in PLANE]


def depth_peers():
    return [along(step) for step in DEPTH]


AROUND = [(-1, -1), (-1, 1), (1, -1), (1, 1), (0, -1), (0, 1), (-1, 0), (1, 0)]


def each(count, body):
    def step(k, carry):
        body(k)
        return carry

    lax.fori_loop(0, count, step, 0)


def along(dz):
    r, c = spot()
    return r, lax.rem(c // 2 + 16 + dz, 16) * 2 + lax.rem(c, 2)


def tell(semaphore, device):
    pl.semaphore_signal(semaphore, inc=1, device_id=device, device_id_type=MESH)


def enter():
    barrier = pltpu.get_barrier_semaphore()
    for dr, dc in AROUND:
        tell(barrier, beside(dr, dc))
    for device in plane_peers():
        tell(barrier, device)
    for dz in (1, -1):
        tell(barrier, along(dz))


def entered():
    pl.semaphore_wait(pltpu.get_barrier_semaphore(), 8 + 31 + 2)


def dot(a, b):
    return jnp.dot(a, b, preferred_element_type=F32)


def gate(v):
    return v * jnp.minimum(jnp.maximum(v + 3.0, 0.0), 6.0)


def inside(rows, halo, lanes):
    r, c = spot()
    at = lax.broadcasted_iota(jnp.int32, (rows * PITCH, lanes), 0)
    row = at // PITCH
    col = at - row * PITCH
    row = row + (r * ROWS - halo)
    col = col + (c * COLS - halo)
    ok = (row >= 0) & (row < 128) & (col >= 0) & (col < 1024)
    return jnp.where(ok, 1.0, 0.0).astype(F32)


def pack(tile, left, right, packed, wide):
    for r in range(ROWS):
        row = tile(r)
        packed[0, 4 * r : 4 * r + 4, :wide] = row[0:4]
        packed[1, 4 * r : 4 * r + 4, :wide] = row[COLS - 4 : COLS]
    left[...] = packed[0, :, :wide].astype(BF16)
    right[...] = packed[1, :, :wide].astype(BF16)


def trade(tile, left, right, halo, across, sides, corners, send, recv):
    low = tile.at[pl.ds(ROWS - halo, halo)]
    high = tile.at[pl.ds(0, halo)]
    top = pl.ds(0, 16)
    bottom = pl.ds(16, 16)
    plan = [
        ((1, 1), right.at[bottom], corners.at[0]),
        ((1, -1), left.at[bottom], corners.at[1]),
        ((-1, 1), right.at[top], corners.at[2]),
        ((-1, -1), left.at[top], corners.at[3]),
        ((0, 1), right, sides.at[0]),
        ((0, -1), left, sides.at[1]),
        ((1, 0), low, across.at[0]),
        ((-1, 0), high, across.at[1]),
    ]
    return [
        pltpu.make_async_remote_copy(
            src_ref=src,
            dst_ref=dst,
            send_sem=send.at[i],
            recv_sem=recv.at[i],
            device_id=beside(*where),
            device_id_type=MESH,
        )
        for i, (where, src, dst) in enumerate(plan)
    ]


def assemble(out, tile, halo, across, sides, corners):
    wide = out.shape[1]
    skip = 4 - halo
    ends = halo + COLS

    def put(row, col, value):
        start = row * PITCH + col
        out[start : start + value.shape[0], :] = value

    for r in range(ROWS):
        put(halo + r, halo, tile[r].astype(F32))
    for r in range(halo):
        put(r, halo, across[0, r].astype(F32))
        put(halo + ROWS + r, halo, across[1, r].astype(F32))
    west = sides[0].astype(F32)
    east = sides[1].astype(F32)
    for r in range(ROWS):
        put(halo + r, 0, west[4 * r + skip : 4 * r + 4])
        put(halo + r, ends, east[4 * r : 4 * r + halo])
    nw, ne, sw, se = [corners[i].astype(F32) for i in range(4)]
    for r in range(halo):
        low = 4 * (r + skip)
        put(r, 0, nw[low + skip : low + 4])
        put(r, ends, ne[low : low + halo])
        put(halo + ROWS + r, 0, sw[4 * r + skip : 4 * r + 4])
        put(halo + ROWS + r, ends, se[4 * r : 4 * r + halo])


def prepare(qkv_weight, agg_depth, agg_group, qkv_w, agg_w, grp_w, stack):
    i = lax.broadcasted_iota(jnp.int32, (3 * WIDTH, 3 * WIDTH), 0)
    j = lax.broadcasted_iota(jnp.int32, (3 * WIDTH, 3 * WIDTH), 1)
    kind = j // WIDTH
    head = (j - kind * WIDTH) // HD
    lane = j - (j // HD) * HD
    order = jnp.where(i == head * (3 * HD) + kind * HD + lane, 1.0, 0.0).astype(BF16)
    stack[...] = jnp.zeros_like(stack)
    for s in range(2):
        qkv_w[s] = dot(qkv_weight[s], order).astype(BF16)
        for a in range(5):
            for b in range(5):
                at = 40 * s + 8 * a + b
                stack[at : at + 1] = agg_depth[a, b, s : s + 1]
    full = stack[...]
    high = full.astype(BF16)
    rest = full - high.astype(F32)
    mid = rest.astype(BF16)
    low = (rest - mid.astype(F32)).astype(BF16)
    moved = dot(high, order) + dot(mid, order) + dot(low, order)
    i = lax.broadcasted_iota(jnp.int32, (HD, WIDTH), 0)
    j = lax.broadcasted_iota(jnp.int32, (HD, WIDTH), 1)
    spread = jnp.where(i == j - (j // HD) * HD, 1.0, 0.0).astype(BF16)
    i = lax.broadcasted_iota(jnp.int32, (WIDTH, WIDTH), 0)
    j = lax.broadcasted_iota(jnp.int32, (WIDTH, WIDTH), 1)
    same = i // HD == j // HD
    for s in range(2):
        agg_w[s] = moved[40 * s : 40 * s + 40]
        for t in range(3):
            rows = jnp.concatenate([agg_group[s, 3 * h + t] for h in range(HEADS)], axis=0)
            grp_w[s, t] = jnp.where(same, dot(rows, spread), 0.0).astype(BF16)


def kernel(*refs):
    given, (out_map, out_boxes), held = refs[:14], refs[14:16], refs[16:30]
    (
        features,
        expand_weight,
        expand_bias,
        depth_weight,
        depth_bias,
        project_weight,
        project_bias,
        qkv_weight,
        agg_depth,
        agg_group,
        output_weight,
        output_bias,
        head_weight,
        head_bias,
    ) = held
    (
        xp,
        xb,
        edge3,
        edge2,
        hidden,
        spread,
        acc,
        qkv,
        scaled,
        center,
        mixed,
        joined,
        asked,
        blocks01,
        unit,
        qkv_w,
        agg_w,
        grp_w,
        stack,
        head_w,
        packed,
        lefts,
        rights,
        f_left,
        f_right,
        tile,
        f_across,
        f_sides,
        f_corners,
        across3,
        across1,
        sides,
        corners,
        part,
        got,
        mine,
        deep,
        total,
        whole,
        table,
        keys,
        hs_send,
        hs_recv,
        ar_send,
        ar_recv,
        ring,
        load,
    ) = refs[30:]
    loads = [
        pltpu.make_async_copy(src, dst, load.at[i]) for i, (src, dst) in enumerate(zip(given, held))
    ]
    loads[0].start()
    enter()
    loads[0].wait()
    pack(lambda r: features[r].astype(F32), f_left, f_right, packed, WIDTH)
    entered()
    first = trade(
        features, f_left, f_right, 3, f_across, f_sides, f_corners, hs_send.at[2], hs_recv.at[2]
    )
    for copy in first:
        copy.start()
    for copy in loads[1:]:
        copy.start()
    for dz in (1, -1):
        tell(ring.at[0], along(dz))
    xp[...] = jnp.zeros_like(xp)
    joined[...] = jnp.zeros_like(joined)
    part[...] = jnp.zeros_like(part)
    head_w[...] = jnp.zeros_like(head_w)
    edge3[...] = inside(14, 3, 128) * (1.0 / 6.0)
    edge2[...] = inside(12, 2, 128)
    i = lax.broadcasted_iota(jnp.int32, (WIDTH, WIDTH), 0)
    j = lax.broadcasted_iota(jnp.int32, (WIDTH, WIDTH), 1)
    blocks01[...] = jnp.where(i // HD == j // HD, 1.0, 0.0)
    unit[...] = jnp.where(i == j, 1.0, 0.0)
    for copy in loads[1:]:
        copy.wait()
    prepare(qkv_weight, agg_depth, agg_group, qkv_w, agg_w, grp_w, stack)
    for a in range(3):
        for b in range(3):
            at = 8 * (3 * a + b)
            head_w[at : at + 4] = head_weight[a, b].astype(F32)
    pl.semaphore_wait(ring.at[0], 2)
    for dz in (2, -2):
        tell(ring.at[1], along(dz))
    for copy in first:
        copy.wait()
    assemble(xp, features, 3, f_across, f_sides, f_corners)
    xb[...] = xp[...].astype(BF16)

    for s in range(2):
        halo = HALOS[s]
        def grow(c, lanes, s=s):
            value = gate(dot(xb[...], expand_weight[s, :, lanes]) + expand_bias[s : s + 1, lanes])
            for l in range(CHUNK // 128):
                hidden[c, :, 128 * l : 128 * l + 128] = (
                    value[:, 128 * l : 128 * l + 128] * edge3[...]
                )

        def filter3(source, lanes, s=s):
            taps = [[depth_weight[a, b, s : s + 1, lanes] for b in range(3)] for a in range(3)]
            bias = depth_bias[s : s + 1, lanes]
            for pair in range(6):
                done = []
                for r in (2 * pair, 2 * pair + 1):
                    rows = [source(PITCH * (r + a)) for a in range(3)]
                    cols = [
                        rows[0] * taps[0][b] + rows[1] * taps[1][b] + rows[2] * taps[2][b]
                        for b in range(3)
                    ]
                    value = (
                        cols[0]
                        + pltpu.roll(cols[1], PITCH - 1, 0)
                        + pltpu.roll(cols[2], PITCH - 2, 0)
                        + bias
                    )
                    done.append(gate(value))
                spread[2 * PITCH * pair : 2 * PITCH * (pair + 1), lanes] = jnp.concatenate(
                    done, axis=0
                ).astype(BF16)

        for c in range(EXPANDED // CHUNK):
            grow(c, slice(c * CHUNK, c * CHUNK + CHUNK))
            for l in range(CHUNK // 128):
                filter3(
                    lambda at, c=c, l=l: hidden[c, at : at + PITCH, 128 * l : 128 * l + 128],
                    slice(c * CHUNK + 128 * l, c * CHUNK + 128 * l + 128),
                )
        acc[...] = dot(spread[...], project_weight[s]) * (1.0 / 6.0)
        if s == 0:
            pl.semaphore_wait(ring.at[1], 2)
            for dz in (4, -4):
                tell(ring.at[2], along(dz))
        bias = project_bias[s : s + 1]
        for r in range(12):
            here = slice(PITCH * r, PITCH * r + PITCH)
            base = xp[PITCH * (r + 1) : PITCH * (r + 2)]
            value = acc[here] + pltpu.roll(base, PITCH - 1, 0) + bias
            for l in range(WIDTH // 128):
                lanes = slice(128 * l, 128 * l + 128)
                mixed[here, lanes] = value[:, lanes] * edge2[here]
        source = mixed[...].astype(BF16)
        qkv[:, WIDTH:] = dot(source, qkv_w[s, :, WIDTH:])

        def taps5(l, s=s):
            lanes = slice(l * 128, l * 128 + 128)
            for r in range(ROWS):
                cols = [None] * 5
                for a in range(5):
                    row = qkv[PITCH * (r + a) : PITCH * (r + a) + PITCH, lanes]
                    for b in range(5):
                        term = row * agg_w[s, 8 * a + b : 8 * a + b + 1, lanes]
                        cols[b] = term if a == 0 else cols[b] + term
                value = cols[0]
                for b in range(1, 5):
                    value = value + pltpu.roll(cols[b], PITCH - b, 0)
                scaled[COLS * r : COLS * r + COLS, lanes] = value[0:COLS].astype(BF16)
                near = pltpu.roll(qkv[PITCH * (r + 2) : PITCH * (r + 3), lanes], PITCH - 2, 0)
                center[COLS * r : COLS * r + COLS, lanes] = near[0:COLS].astype(BF16)

        def kind(t):
            lanes = slice(WIDTH * t, WIDTH * t + WIDTH)
            return [center[:, lanes], dot(scaled[:, lanes], grp_w[s, t]).astype(BF16)]

        for l in range(2, 6):
            taps5(l)
        lane = lax.broadcasted_iota(jnp.int32, (HD, 128), 1) // HD
        ones = jnp.ones((16, ROWS * COLS), BF16)
        for branch, (k, v) in enumerate(zip(kind(1), kind(2))):
            k = jnp.maximum(k, jnp.zeros_like(k))
            outer = lax.dot_general(k, v, (((0,), (0,)), ((), ())), preferred_element_type=F32)
            count = dot(ones, k)
            for g in range(2):
                group = 2 * branch + g
                lanes = slice(128 * g, 128 * g + 128)
                fold = jnp.zeros((HD, 128), F32)
                for h in range(4):
                    low = 128 * g + HD * h
                    fold = jnp.where(lane == h, outer[low : low + HD, lanes], fold)
                for p in range(8):
                    part[s, 8 * group + p, 0:4, :] = fold[4 * p : 4 * p + 4]
                part[s, group, 4:5, :] = count[0:1, lanes]

        me = plane_of(*spot())
        depth = spot()[1] // 2

        def remote(src, dst, stage, device):
            return pltpu.make_async_remote_copy(
                src_ref=src,
                dst_ref=dst,
                send_sem=ar_send.at[s, stage],
                recv_sem=ar_recv.at[s, stage],
                device_id=device,
                device_id_type=MESH,
            )

        def arrived(buffer, count, stage, s=s):
            view = buffer.at[s, pl.ds(0, count)]
            pltpu.make_async_copy(view, view, ar_recv.at[s, stage]).wait()

        def sent(buffer, count, stage, s=s):
            view = buffer.at[s, pl.ds(0, count)]
            pltpu.make_async_copy(view, view, ar_send.at[s, stage]).wait()

        for device in plane_peers():
            remote(part.at[s, plane_of(*device)], got.at[s, me], 0, device).start()
        got[s, me] = part[s, me]

        qkv[:, 0:WIDTH] = dot(mixed[...].astype(BF16), qkv_w[s, :, 0:WIDTH])
        for l in range(2):
            taps5(l)
        near, far = kind(0)
        for r in range(ROWS):
            here = slice(COLS * r, COLS * r + COLS)
            value = pltpu.roll(mixed[PITCH * (r + 2) : PITCH * (r + 3)], PITCH - 2, 0)
            tile[s, r, :, 0:WIDTH] = value[0:COLS].astype(BF16)
            tile[s, r, :, WIDTH : 2 * WIDTH] = jnp.maximum(near[here], jnp.zeros_like(near[here]))
            tile[s, r, :, 2 * WIDTH :] = jnp.maximum(far[here], jnp.zeros_like(far[here]))
        pack(
            lambda r, s=s: tile[s, r].astype(F32), lefts.at[s], rights.at[s], packed, 3 * WIDTH
        )
        across = across3 if halo == 3 else across1
        swap = trade(
            tile.at[s],
            lefts.at[s],
            rights.at[s],
            halo,
            across,
            sides.at[s],
            corners.at[s],
            hs_send.at[s],
            hs_recv.at[s],
        )

        arrived(got, 31, 0)
        mine[s] = jnp.sum(got[s], axis=0)
        if s == 0:
            pl.semaphore_wait(ring.at[2], 2)
        for device in depth_peers():
            remote(mine.at[s], deep.at[s, depth], 1, device).start()
        deep[s, depth] = mine[s]
        for copy in swap:
            copy.start()
        arrived(deep, 15, 1)
        total[s] = jnp.sum(deep[s], axis=0)
        for device in plane_peers():
            remote(total.at[s], whole.at[s, me], 2, device).start()
        whole[s, me] = total[s]
        for copy in swap:
            copy.wait()
        area = (ROWS + 2 * halo) * PITCH
        assemble(joined.at[pl.ds(0, area)], tile.at[s], halo, across, sides.at[s], corners.at[s])
        asked[0:area] = joined[0:area, WIDTH:].astype(BF16)
        arrived(whole, 31, 2)
        sent(got, 31, 0)
        sent(deep, 15, 1)
        sent(whole, 31, 2)

        for p in range(32):
            table[4 * p : 4 * p + 4, :] = whole[s, p, 0:4, :]
        same = blocks01[...]
        ones = same.astype(BF16)
        attended = []
        for branch in range(2):
            blocks = []
            for g in range(2):
                group = 2 * branch + g
                block = table[HD * group : HD * group + HD]
                blocks.append(jnp.concatenate([block] * 4, axis=0))
                keys[0:1, 128 * g : 128 * g + 128] = whole[s, group, 4:5, :]
            numer_w = same * jnp.concatenate(
                [jnp.concatenate([b, b], axis=1) for b in blocks], axis=0
            )
            denom_w = dot((unit[...] * keys[0:1, :]).astype(BF16), ones)
            q = asked[0:area, WIDTH * branch : WIDTH * (branch + 1)]
            numer = dot(q, numer_w.astype(BF16))
            denom = dot(q, denom_w.astype(BF16))
            attended.append((numer / (denom + 1e-06)).astype(BF16))
        value = (
            joined[0:area, 0:WIDTH]
            + dot(attended[0], output_weight[s, 0:WIDTH])
            + dot(attended[1], output_weight[s, WIDTH:])
            + output_bias[s : s + 1]
        )
        xp[0:area] = value
        xb[0:area] = value.astype(BF16)

    for r in range(ROWS):
        start = PITCH * (r + 1) + 1
        out_map[r] = xp[start : start + COLS].astype(BF16)
    area = 10 * PITCH
    on_map = inside(10, 1, 128)
    final = jnp.concatenate(
        [
            (xp[0:area, 128 * l : 128 * l + 128] * on_map).astype(BF16)
            for l in range(WIDTH // 128)
        ],
        axis=1,
    )
    final = jnp.concatenate([final, jnp.zeros((512 - area, WIDTH), BF16)], axis=0)
    taps = lax.dot_general(
        head_w[...].astype(BF16), final, (((1,), (1,)), ((), ())), preferred_element_type=F32
    )
    boxes = jnp.zeros((8, 512), F32)
    for a in range(3):
        for b in range(3):
            at = 8 * (3 * a + b)
            shift = PITCH * a + b
            term = taps[at : at + 8]
            boxes = boxes + (term if shift == 0 else pltpu.roll(term, 512 - shift, 1))
    for r in range(ROWS):
        row = boxes if r == 0 else pltpu.roll(boxes, 512 - PITCH * r, 1)
        for o in range(4):
            out_boxes[o, r : r + 1, :] = row[o : o + 1, 0:COLS] + head_bias[o]


def local(*args):
    args = list(args)
    for i in (3, 8):
        args[i] = jnp.transpose(args[i], (1, 2, 0, 3))
    dma = pltpu.SemaphoreType.DMA
    vmem = pltpu.VMEM
    area = 14 * PITCH
    inner = 12 * PITCH
    wide = 3 * WIDTH
    held = [vmem(a.shape, a.dtype) for a in args[:13]] + [pltpu.SMEM((4,), F32)]
    scratch = held + [
        vmem((area, WIDTH), F32),
        vmem((area, WIDTH), BF16),
        vmem((area, 128), F32),
        vmem((inner, 128), F32),
        vmem((EXPANDED // CHUNK, area, CHUNK), F32),
        vmem((inner, EXPANDED), BF16),
        vmem((inner, WIDTH), F32),
        vmem((inner, wide), F32),
        vmem((ROWS * COLS, wide), BF16),
        vmem((ROWS * COLS, wide), BF16),
        vmem((inner, WIDTH), F32),
        vmem((area, wide), F32),
        vmem((area, 2 * WIDTH), BF16),
        vmem((WIDTH, WIDTH), F32),
        vmem((WIDTH, WIDTH), F32),
        vmem((2, WIDTH, wide), BF16),
        vmem((2, 40, wide), F32),
        vmem((2, 3, WIDTH, WIDTH), BF16),
        vmem((80, wide), F32),
        vmem((72, WIDTH), F32),
        vmem((2, 32, wide), F32),
        vmem((2, 32, wide), BF16),
        vmem((2, 32, wide), BF16),
        vmem((32, WIDTH), BF16),
        vmem((32, WIDTH), BF16),
        vmem((2, ROWS, COLS, wide), BF16),
        vmem((2, 3, COLS, WIDTH), BF16),
        vmem((2, 32, WIDTH), BF16),
        vmem((4, 16, WIDTH), BF16),
        vmem((2, 3, COLS, wide), BF16),
        vmem((2, 1, COLS, wide), BF16),
        vmem((2, 2, 32, wide), BF16),
        vmem((2, 4, 16, wide), BF16),
        vmem((2, 32, 5, 128), F32),
        vmem((2, 32, 5, 128), F32),
        vmem((2, 5, 128), F32),
        vmem((2, 16, 5, 128), F32),
        vmem((2, 5, 128), F32),
        vmem((2, 32, 5, 128), F32),
        vmem((128, 128), F32),
        vmem((8, WIDTH), F32),
        dma((3, 8)),
        dma((3, 8)),
        dma((2, 3)),
        dma((2, 3)),
        pltpu.SemaphoreType.REGULAR((3,)),
        dma((14,)),
    ]
    in_vmem = pl.BlockSpec(memory_space=pltpu.VMEM)
    return pl.pallas_call(
        kernel,
        out_shape=(
            jax.ShapeDtypeStruct((ROWS, COLS, WIDTH), BF16),
            jax.ShapeDtypeStruct((4, ROWS, COLS), F32),
        ),
        in_specs=[pl.BlockSpec(memory_space=pl.ANY)] * 14,
        out_specs=(in_vmem, in_vmem),
        scratch_shapes=scratch,
        compiler_params=pltpu.CompilerParams(
            collective_id=0, has_side_effects=True, vmem_limit_bytes=60 * 1024 * 1024
        ),
    )(*args)


def solution(mesh):
    return jax.shard_map(
        local,
        mesh=mesh,
        in_specs=(P("row", "col", None),) + (P(),) * 13,
        out_specs=(P("row", "col", None), P(None, "row", "col")),
        check_vma=False,
    )
```

```python
import functools

import jax
import jax.numpy as jnp
from jax import lax
from jax.experimental import pallas as pl
from jax.experimental.pallas import tpu as pltpu
from jax.sharding import PartitionSpec as P

MESH = pl.DeviceIdType.MESH
F32 = jnp.float32
BF16 = jnp.bfloat16
ROWS = 8
COLS = 32
PITCH = 40
WIDTH = 256
EXPANDED = 1024
CHUNK = 256
HD = 32
HEADS = 8
HALOS = (3, 1)


def spot():
    return lax.axis_index("row"), lax.axis_index("col")


def beside(dr, dc):
    r, c = spot()
    return lax.rem(r + 16 + dr, 16), lax.rem(c + 32 + dc, 32)


def plane_of(r, c):
    return r * 2 + lax.rem(c, 2)


def hops(step, around):
    return min(step, around - step)


PLANE = sorted(
    [(x, y, k) for x in range(4) for y in range(4) for k in range(2) if x or y or k],
    key=lambda step: -hops(step[0], 4) - hops(step[1], 4),
)
DEPTH = sorted(range(1, 16), key=lambda step: -hops(step, 16))


def plane_peers():
    r, c = spot()
    y = lax.rem(c, 2) * 2 + lax.rem(r // 2, 2)
    k = lax.rem(r, 2)
    first = [lax.rem(r // 4 + step, 4) * 4 for step in range(4)]
    ys = [lax.rem(y + step, 4) for step in range(4)]
    second = [lax.rem(at, 2) * 2 for at in ys]
    cols = [(c // 2) * 2 + at // 2 for at in ys]
    cores = [k, 1 - k]
    return [(first[x] + second[y] + cores[k], cols[y]) for x, y, k in PLANE]


def depth_peers():
    return [along(step) for step in DEPTH]


AROUND = [(-1, -1), (-1, 1), (1, -1), (1, 1), (0, -1), (0, 1), (-1, 0), (1, 0)]


def each(count, body):
    def step(k, carry):
        body(k)
        return carry

    lax.fori_loop(0, count, step, 0)


def along(dz):
    r, c = spot()
    return r, lax.rem(c // 2 + 16 + dz, 16) * 2 + lax.rem(c, 2)


def tell(semaphore, device):
    pl.semaphore_signal(semaphore, inc=1, device_id=device, device_id_type=MESH)


def enter():
    barrier = pltpu.get_barrier_semaphore()
    for dr, dc in AROUND:
        tell(barrier, beside(dr, dc))
    for device in plane_peers():
        tell(barrier, device)
    for dz in (1, -1):
        tell(barrier, along(dz))


def entered():
    pl.semaphore_wait(pltpu.get_barrier_semaphore(), 8 + 31 + 2)


def dot(a, b):
    return jnp.dot(a, b, preferred_element_type=F32)


def gate(v):
    return v * jnp.minimum(jnp.maximum(v + 3.0, 0.0), 6.0)


def inside(rows, halo, lanes):
    r, c = spot()
    at = lax.broadcasted_iota(jnp.int32, (rows * PITCH, lanes), 0)
    row = at // PITCH
    col = at - row * PITCH
    row = row + (r * ROWS - halo)
    col = col + (c * COLS - halo)
    ok = (row >= 0) & (row < 128) & (col >= 0) & (col < 1024)
    return jnp.where(ok, 1.0, 0.0).astype(F32)


def pack(tile, left, right, packed, wide):
    for r in range(ROWS):
        row = tile(r)
        packed[0, 4 * r : 4 * r + 4, :wide] = row[0:4]
        packed[1, 4 * r : 4 * r + 4, :wide] = row[COLS - 4 : COLS]
    left[...] = packed[0, :, :wide].astype(BF16)
    right[...] = packed[1, :, :wide].astype(BF16)


def trade(tile, left, right, halo, across, sides, corners, send, recv):
    low = tile.at[pl.ds(ROWS - halo, halo)]
    high = tile.at[pl.ds(0, halo)]
    top = pl.ds(0, 16)
    bottom = pl.ds(16, 16)
    plan = [
        ((1, 1), right.at[bottom], corners.at[0]),
        ((1, -1), left.at[bottom], corners.at[1]),
        ((-1, 1), right.at[top], corners.at[2]),
        ((-1, -1), left.at[top], corners.at[3]),
        ((0, 1), right, sides.at[0]),
        ((0, -1), left, sides.at[1]),
        ((1, 0), low, across.at[0]),
        ((-1, 0), high, across.at[1]),
    ]
    return [
        pltpu.make_async_remote_copy(
            src_ref=src,
            dst_ref=dst,
            send_sem=send.at[i],
            recv_sem=recv.at[i],
            device_id=beside(*where),
            device_id_type=MESH,
        )
        for i, (where, src, dst) in enumerate(plan)
    ]


def assemble(out, tile, halo, across, sides, corners):
    wide = out.shape[1]
    skip = 4 - halo
    ends = halo + COLS

    def put(row, col, value):
        start = row * PITCH + col
        out[start : start + value.shape[0], :] = value

    for r in range(ROWS):
        put(halo + r, halo, tile[r].astype(F32))
    for r in range(halo):
        put(r, halo, across[0, r].astype(F32))
        put(halo + ROWS + r, halo, across[1, r].astype(F32))
    west = sides[0].astype(F32)
    east = sides[1].astype(F32)
    for r in range(ROWS):
        put(halo + r, 0, west[4 * r + skip : 4 * r + 4])
        put(halo + r, ends, east[4 * r : 4 * r + halo])
    nw, ne, sw, se = [corners[i].astype(F32) for i in range(4)]
    for r in range(halo):
        low = 4 * (r + skip)
        put(r, 0, nw[low + skip : low + 4])
        put(r, ends, ne[low : low + halo])
        put(halo + ROWS + r, 0, sw[4 * r + skip : 4 * r + 4])
        put(halo + ROWS + r, ends, se[4 * r : 4 * r + halo])


def prepare(qkv_weight, agg_depth, agg_group, qkv_w, agg_w, grp_w, stack):
    i = lax.broadcasted_iota(jnp.int32, (3 * WIDTH, 3 * WIDTH), 0)
    j = lax.broadcasted_iota(jnp.int32, (3 * WIDTH, 3 * WIDTH), 1)
    kind = j // WIDTH
    head = (j - kind * WIDTH) // HD
    lane = j - (j // HD) * HD
    order = jnp.where(i == head * (3 * HD) + kind * HD + lane, 1.0, 0.0).astype(BF16)
    stack[...] = jnp.zeros_like(stack)
    for s in range(2):
        qkv_w[s] = dot(qkv_weight[s], order).astype(BF16)
        for a in range(5):
            for b in range(5):
                at = 40 * s + 8 * a + b
                stack[at : at + 1] = agg_depth[a, b, s : s + 1]
    full = stack[...]
    high = full.astype(BF16)
    rest = full - high.astype(F32)
    mid = rest.astype(BF16)
    low = (rest - mid.astype(F32)).astype(BF16)
    moved = dot(high, order) + dot(mid, order) + dot(low, order)
    i = lax.broadcasted_iota(jnp.int32, (HD, WIDTH), 0)
    j = lax.broadcasted_iota(jnp.int32, (HD, WIDTH), 1)
    spread = jnp.where(i == j - (j // HD) * HD, 1.0, 0.0).astype(BF16)
    i = lax.broadcasted_iota(jnp.int32, (WIDTH, WIDTH), 0)
    j = lax.broadcasted_iota(jnp.int32, (WIDTH, WIDTH), 1)
    same = i // HD == j // HD
    for s in range(2):
        agg_w[s] = moved[40 * s : 40 * s + 40]
        for t in range(3):
            rows = jnp.concatenate([agg_group[s, 3 * h + t] for h in range(HEADS)], axis=0)
            grp_w[s, t] = jnp.where(same, dot(rows, spread), 0.0).astype(BF16)


def kernel(*refs):
    given, (out_map, out_boxes), held = refs[:14], refs[14:16], refs[16:30]
    (
        features,
        expand_weight,
        expand_bias,
        depth_weight,
        depth_bias,
        project_weight,
        project_bias,
        qkv_weight,
        agg_depth,
        agg_group,
        output_weight,
        output_bias,
        head_weight,
        head_bias,
    ) = held
    (
        xp,
        xb,
        edge3,
        edge2,
        hidden,
        spread,
        acc,
        qkv,
        scaled,
        center,
        mixed,
        joined,
        asked,
        blocks01,
        unit,
        qkv_w,
        agg_w,
        grp_w,
        stack,
        head_w,
        packed,
        lefts,
        rights,
        f_left,
        f_right,
        tile,
        f_across,
        f_sides,
        f_corners,
        across3,
        across1,
        sides,
        corners,
        part,
        got,
        mine,
        deep,
        total,
        whole,
        table,
        keys,
        hs_send,
        hs_recv,
        ar_send,
        ar_recv,
        ring,
        load,
    ) = refs[30:]
    loads = [
        pltpu.make_async_copy(src, dst, load.at[i]) for i, (src, dst) in enumerate(zip(given, held))
    ]
    loads[0].start()
    enter()
    loads[0].wait()
    pack(lambda r: features[r].astype(F32), f_left, f_right, packed, WIDTH)
    entered()
    first = trade(
        features, f_left, f_right, 3, f_across, f_sides, f_corners, hs_send.at[2], hs_recv.at[2]
    )
    for copy in first:
        copy.start()
    for copy in loads[1:]:
        copy.start()
    for dz in (1, -1):
        tell(ring.at[0], along(dz))
    xp[...] = jnp.zeros_like(xp)
    joined[...] = jnp.zeros_like(joined)
    part[...] = jnp.zeros_like(part)
    head_w[...] = jnp.zeros_like(head_w)
    edge3[...] = inside(14, 3, 128) * (1.0 / 6.0)
    edge2[...] = inside(12, 2, 128)
    i = lax.broadcasted_iota(jnp.int32, (WIDTH, WIDTH), 0)
    j = lax.broadcasted_iota(jnp.int32, (WIDTH, WIDTH), 1)
    blocks01[...] = jnp.where(i // HD == j // HD, 1.0, 0.0)
    unit[...] = jnp.where(i == j, 1.0, 0.0)
    for copy in loads[1:]:
        copy.wait()
    prepare(qkv_weight, agg_depth, agg_group, qkv_w, agg_w, grp_w, stack)
    for a in range(3):
        for b in range(3):
            at = 8 * (3 * a + b)
            head_w[at : at + 4] = head_weight[a, b].astype(F32)
    pl.semaphore_wait(ring.at[0], 2)
    for dz in (2, -2):
        tell(ring.at[1], along(dz))
    for copy in first:
        copy.wait()
    assemble(xp, features, 3, f_across, f_sides, f_corners)
    xb[...] = xp[...].astype(BF16)

    for s in range(2):
        halo = HALOS[s]
        def grow(c, lanes, s=s):
            value = gate(dot(xb[...], expand_weight[s, :, lanes]) + expand_bias[s : s + 1, lanes])
            for l in range(CHUNK // 128):
                hidden[c, :, 128 * l : 128 * l + 128] = (
                    value[:, 128 * l : 128 * l + 128] * edge3[...]
                )

        def filter3(source, lanes, s=s):
            taps = [[depth_weight[a, b, s : s + 1, lanes] for b in range(3)] for a in range(3)]
            bias = depth_bias[s : s + 1, lanes]
            for pair in range(6):
                done = []
                for r in (2 * pair, 2 * pair + 1):
                    rows = [source(PITCH * (r + a)) for a in range(3)]
                    cols = [
                        rows[0] * taps[0][b] + rows[1] * taps[1][b] + rows[2] * taps[2][b]
                        for b in range(3)
                    ]
                    value = (
                        cols[0]
                        + pltpu.roll(cols[1], PITCH - 1, 0)
                        + pltpu.roll(cols[2], PITCH - 2, 0)
                        + bias
                    )
                    done.append(gate(value))
                spread[2 * PITCH * pair : 2 * PITCH * (pair + 1), lanes] = jnp.concatenate(
                    done, axis=0
                ).astype(BF16)

        for c in range(EXPANDED // CHUNK):
            grow(c, slice(c * CHUNK, c * CHUNK + CHUNK))
            for l in range(CHUNK // 128):
                filter3(
                    lambda at, c=c, l=l: hidden[c, at : at + PITCH, 128 * l : 128 * l + 128],
                    slice(c * CHUNK + 128 * l, c * CHUNK + 128 * l + 128),
                )
        acc[...] = dot(spread[...], project_weight[s]) * (1.0 / 6.0)
        if s == 0:
            pl.semaphore_wait(ring.at[1], 2)
            for dz in (4, -4):
                tell(ring.at[2], along(dz))
        bias = project_bias[s : s + 1]
        for r in range(12):
            here = slice(PITCH * r, PITCH * r + PITCH)
            base = xp[PITCH * (r + 1) : PITCH * (r + 2)]
            value = acc[here] + pltpu.roll(base, PITCH - 1, 0) + bias
            for l in range(WIDTH // 128):
                lanes = slice(128 * l, 128 * l + 128)
                mixed[here, lanes] = value[:, lanes] * edge2[here]
        source = mixed[...].astype(BF16)
        qkv[:, WIDTH:] = dot(source, qkv_w[s, :, WIDTH:])

        def taps5(l, carry, s=s):
            lanes = pl.ds(pl.multiple_of(l * 128, 128), 128)
            for r in range(ROWS):
                cols = [None] * 5
                for a in range(5):
                    row = qkv[PITCH * (r + a) : PITCH * (r + a) + PITCH, lanes]
                    for b in range(5):
                        term = row * agg_w[s, 8 * a + b : 8 * a + b + 1, lanes]
                        cols[b] = term if a == 0 else cols[b] + term
                value = cols[0]
                for b in range(1, 5):
                    value = value + pltpu.roll(cols[b], PITCH - b, 0)
                scaled[COLS * r : COLS * r + COLS, lanes] = value[0:COLS].astype(BF16)
                near = pltpu.roll(qkv[PITCH * (r + 2) : PITCH * (r + 3), lanes], PITCH - 2, 0)
                center[COLS * r : COLS * r + COLS, lanes] = near[0:COLS].astype(BF16)
            return carry

        def kind(t):
            lanes = slice(WIDTH * t, WIDTH * t + WIDTH)
            return [center[:, lanes], dot(scaled[:, lanes], grp_w[s, t]).astype(BF16)]

        lax.fori_loop(2, 6, taps5, 0)
        lane = lax.broadcasted_iota(jnp.int32, (HD, 128), 1) // HD
        ones = jnp.ones((16, ROWS * COLS), BF16)
        for branch, (k, v) in enumerate(zip(kind(1), kind(2))):
            k = jnp.maximum(k, jnp.zeros_like(k))
            outer = lax.dot_general(k, v, (((0,), (0,)), ((), ())), preferred_element_type=F32)
            count = dot(ones, k)
            for g in range(2):
                group = 2 * branch + g
                lanes = slice(128 * g, 128 * g + 128)
                fold = jnp.zeros((HD, 128), F32)
                for h in range(4):
                    low = 128 * g + HD * h
                    fold = jnp.where(lane == h, outer[low : low + HD, lanes], fold)
                for p in range(8):
                    part[s, 8 * group + p, 0:4, :] = fold[4 * p : 4 * p + 4]
                part[s, group, 4:5, :] = count[0:1, lanes]

        me = plane_of(*spot())
        depth = spot()[1] // 2

        def remote(src, dst, stage, device):
            return pltpu.make_async_remote_copy(
                src_ref=src,
                dst_ref=dst,
                send_sem=ar_send.at[s, stage],
                recv_sem=ar_recv.at[s, stage],
                device_id=device,
                device_id_type=MESH,
            )

        def arrived(buffer, count, stage, s=s):
            view = buffer.at[s, pl.ds(0, count)]
            pltpu.make_async_copy(view, view, ar_recv.at[s, stage]).wait()

        def sent(buffer, count, stage, s=s):
            view = buffer.at[s, pl.ds(0, count)]
            pltpu.make_async_copy(view, view, ar_send.at[s, stage]).wait()

        for device in plane_peers():
            remote(part.at[s, plane_of(*device)], got.at[s, me], 0, device).start()
        got[s, me] = part[s, me]

        qkv[:, 0:WIDTH] = dot(mixed[...].astype(BF16), qkv_w[s, :, 0:WIDTH])
        lax.fori_loop(0, 2, taps5, 0)
        near, far = kind(0)
        for r in range(ROWS):
            here = slice(COLS * r, COLS * r + COLS)
            value = pltpu.roll(mixed[PITCH * (r + 2) : PITCH * (r + 3)], PITCH - 2, 0)
            tile[s, r, :, 0:WIDTH] = value[0:COLS].astype(BF16)
            tile[s, r, :, WIDTH : 2 * WIDTH] = jnp.maximum(near[here], jnp.zeros_like(near[here]))
            tile[s, r, :, 2 * WIDTH :] = jnp.maximum(far[here], jnp.zeros_like(far[here]))
        pack(
            lambda r, s=s: tile[s, r].astype(F32), lefts.at[s], rights.at[s], packed, 3 * WIDTH
        )
        across = across3 if halo == 3 else across1
        swap = trade(
            tile.at[s],
            lefts.at[s],
            rights.at[s],
            halo,
            across,
            sides.at[s],
            corners.at[s],
            hs_send.at[s],
            hs_recv.at[s],
        )

        arrived(got, 31, 0)
        mine[s] = jnp.sum(got[s], axis=0)
        if s == 0:
            pl.semaphore_wait(ring.at[2], 2)
        for device in depth_peers():
            remote(mine.at[s], deep.at[s, depth], 1, device).start()
        deep[s, depth] = mine[s]
        for copy in swap:
            copy.start()
        arrived(deep, 15, 1)
        total[s] = jnp.sum(deep[s], axis=0)
        for device in plane_peers():
            remote(total.at[s], whole.at[s, me], 2, device).start()
        whole[s, me] = total[s]
        for copy in swap:
            copy.wait()
        area = (ROWS + 2 * halo) * PITCH
        assemble(joined.at[pl.ds(0, area)], tile.at[s], halo, across, sides.at[s], corners.at[s])
        asked[0:area] = joined[0:area, WIDTH:].astype(BF16)
        arrived(whole, 31, 2)
        sent(got, 31, 0)
        sent(deep, 15, 1)
        sent(whole, 31, 2)

        for p in range(32):
            table[4 * p : 4 * p + 4, :] = whole[s, p, 0:4, :]
        same = blocks01[...]
        ones = same.astype(BF16)
        attended = []
        for branch in range(2):
            blocks = []
            for g in range(2):
                group = 2 * branch + g
                block = table[HD * group : HD * group + HD]
                blocks.append(jnp.concatenate([block] * 4, axis=0))
                keys[0:1, 128 * g : 128 * g + 128] = whole[s, group, 4:5, :]
            numer_w = same * jnp.concatenate(
                [jnp.concatenate([b, b], axis=1) for b in blocks], axis=0
            )
            denom_w = dot((unit[...] * keys[0:1, :]).astype(BF16), ones)
            q = asked[0:area, WIDTH * branch : WIDTH * (branch + 1)]
            numer = dot(q, numer_w.astype(BF16))
            denom = dot(q, denom_w.astype(BF16))
            attended.append((numer / (denom + 1e-06)).astype(BF16))
        value = (
            joined[0:area, 0:WIDTH]
            + dot(attended[0], output_weight[s, 0:WIDTH])
            + dot(attended[1], output_weight[s, WIDTH:])
            + output_bias[s : s + 1]
        )
        xp[0:area] = value
        xb[0:area] = value.astype(BF16)

    for r in range(ROWS):
        start = PITCH * (r + 1) + 1
        out_map[r] = xp[start : start + COLS].astype(BF16)
    area = 10 * PITCH
    on_map = inside(10, 1, 128)
    final = jnp.concatenate(
        [
            (xp[0:area, 128 * l : 128 * l + 128] * on_map).astype(BF16)
            for l in range(WIDTH // 128)
        ],
        axis=1,
    )
    final = jnp.concatenate([final, jnp.zeros((512 - area, WIDTH), BF16)], axis=0)
    taps = lax.dot_general(
        head_w[...].astype(BF16), final, (((1,), (1,)), ((), ())), preferred_element_type=F32
    )
    boxes = jnp.zeros((8, 512), F32)
    for a in range(3):
        for b in range(3):
            at = 8 * (3 * a + b)
            shift = PITCH * a + b
            term = taps[at : at + 8]
            boxes = boxes + (term if shift == 0 else pltpu.roll(term, 512 - shift, 1))
    for r in range(ROWS):
        row = boxes if r == 0 else pltpu.roll(boxes, 512 - PITCH * r, 1)
        for o in range(4):
            out_boxes[o, r : r + 1, :] = row[o : o + 1, 0:COLS] + head_bias[o]


def local(*args):
    args = list(args)
    for i in (3, 8):
        args[i] = jnp.transpose(args[i], (1, 2, 0, 3))
    dma = pltpu.SemaphoreType.DMA
    vmem = pltpu.VMEM
    area = 14 * PITCH
    inner = 12 * PITCH
    wide = 3 * WIDTH
    held = [vmem(a.shape, a.dtype) for a in args[:13]] + [pltpu.SMEM((4,), F32)]
    scratch = held + [
        vmem((area, WIDTH), F32),
        vmem((area, WIDTH), BF16),
        vmem((area, 128), F32),
        vmem((inner, 128), F32),
        vmem((EXPANDED // CHUNK, area, CHUNK), F32),
        vmem((inner, EXPANDED), BF16),
        vmem((inner, WIDTH), F32),
        vmem((inner, wide), F32),
        vmem((ROWS * COLS, wide), BF16),
        vmem((ROWS * COLS, wide), BF16),
        vmem((inner, WIDTH), F32),
        vmem((area, wide), F32),
        vmem((area, 2 * WIDTH), BF16),
        vmem((WIDTH, WIDTH), F32),
        vmem((WIDTH, WIDTH), F32),
        vmem((2, WIDTH, wide), BF16),
        vmem((2, 40, wide), F32),
        vmem((2, 3, WIDTH, WIDTH), BF16),
        vmem((80, wide), F32),
        vmem((72, WIDTH), F32),
        vmem((2, 32, wide), F32),
        vmem((2, 32, wide), BF16),
        vmem((2, 32, wide), BF16),
        vmem((32, WIDTH), BF16),
        vmem((32, WIDTH), BF16),
        vmem((2, ROWS, COLS, wide), BF16),
        vmem((2, 3, COLS, WIDTH), BF16),
        vmem((2, 32, WIDTH), BF16),
        vmem((4, 16, WIDTH), BF16),
        vmem((2, 3, COLS, wide), BF16),
        vmem((2, 1, COLS, wide), BF16),
        vmem((2, 2, 32, wide), BF16),
        vmem((2, 4, 16, wide), BF16),
        vmem((2, 32, 5, 128), F32),
        vmem((2, 32, 5, 128), F32),
        vmem((2, 5, 128), F32),
        vmem((2, 16, 5, 128), F32),
        vmem((2, 5, 128), F32),
        vmem((2, 32, 5, 128), F32),
        vmem((128, 128), F32),
        vmem((8, WIDTH), F32),
        dma((3, 8)),
        dma((3, 8)),
        dma((2, 3)),
        dma((2, 3)),
        pltpu.SemaphoreType.REGULAR((3,)),
        dma((14,)),
    ]
    in_vmem = pl.BlockSpec(memory_space=pltpu.VMEM)
    return pl.pallas_call(
        kernel,
        out_shape=(
            jax.ShapeDtypeStruct((ROWS, COLS, WIDTH), BF16),
            jax.ShapeDtypeStruct((4, ROWS, COLS), F32),
        ),
        in_specs=[pl.BlockSpec(memory_space=pl.ANY)] * 14,
        out_specs=(in_vmem, in_vmem),
        scratch_shapes=scratch,
        compiler_params=pltpu.CompilerParams(
            collective_id=0, has_side_effects=True, vmem_limit_bytes=60 * 1024 * 1024
        ),
    )(*args)


def solution(mesh):
    return jax.shard_map(
        local,
        mesh=mesh,
        in_specs=(P("row", "col", None),) + (P(),) * 13,
        out_specs=(P("row", "col", None), P(None, "row", "col")),
        check_vma=False,
    )
```
